32 devices in a mesh: groups: 2 (over x), attn: 16 (over z, y, core).
Axes of the slice: x: 2, y: 2, z: 4, core: 2. Of those that a mesh axis runs over, the one named last changes fastest.
Arguments:
- queries: bfloat16 [512, 3072], P(('groups', 'attn')), parts along dimension 0, may hold values from -6 to 6
- residual: bfloat16 [512, 3072], P(('groups', 'attn')), parts along dimension 0, may hold values from -36 to 36
- key_cache: bfloat16 [512, 96, 512], P(('groups', 'attn')), parts along dimension 0, may hold values from -6 to 6
- value_cache: bfloat16 [512, 96, 512], P(('groups', 'attn')), parts along dimension 0, may hold values from -6 to 6
- new_keys: bfloat16 [512, 512], P(('groups', 'attn')), parts along dimension 0, may hold values from -6 to 6
- new_values: bfloat16 [512, 512], P(('groups', 'attn')), parts along dimension 0, may hold values from -6 to 6
- cache_len: int32 [512], P(('groups', 'attn')), parts along dimension 0, may hold values from 1 to 96, 12288 in all
- norm_gain: float32 [3072], replicated, may hold values from 0.5 to 1.5
- expert_ids: int32 [512, 2], P(('groups', 'attn')), parts along dimension 0, may hold values from 0 to 3, all different within a row; in each aligned block of 8 rows (0 to 7, 8 to 15, ...) at most 6 rows name the same one
- gate_fixed: int32 [512, 2], P(('groups', 'attn')), parts along dimension 0, may hold values from 1 to 4096
- gate_weight: bfloat16 [3072, 32768], P(None, 'attn'), may hold values from -0.109375 to 0.109375
- up_weight: bfloat16 [3072, 32768], P(None, 'attn'), may hold values from -0.109375 to 0.109375
- down_weight: bfloat16 [32768, 3072], P('attn'), may hold values from -0.0625 to 0.0625
Outputs:
- mixed: bfloat16 [512, 3072], P(('groups', 'attn')), parts along dimension 0
The draws below stay inside these ranges and needn't reach their ends.
There are 2 independent parts, one for each index of `groups`. The reference program is written for one: setup_inputs(seed, part) draws one part's arguments, and reference() takes and returns one part's arrays. A program takes and returns all parts, laid end to end along the dimension named above; an argument that names none is the same for every part. Nothing has to cross between parts.
Inputs may be any that keep to these rules, and one draw needn't show every extreme that they name: `cache_len`: slots in use of each sequence. Within each part (each replica's 256 sequences) the lengths sum to 12288, and some sequence of the part uses all 96; the whole array over all parts sums to that total times the number of parts. `expert_ids`: the 2 experts of a token differ. In each aligned block of 8 rows (one device's micro-batch) no expert is named by more than 6 rows, and in every draw some block has an expert named by exactly 6 rows. `gate_fixed`: A routing weight is the value divided by 4096.
All inputs are finite; a program needn't handle non-finite values. No bound on the sum of `cache_len` on one device may be relied on, other than what follows from the above.
Results may differ from the reference program's by a relative error of at most 0.0057.
Values may be sent and summed in bfloat16 or wider, within the bound.
No kernel may reach another device: no remote copies, remote signals or barrier semaphores. Data moves between devices by JAX's collectives and lax.ppermute only.
A program may use at most 128 MiB of HBM per device.

```python
import math
import jax
import jax.numpy as jnp
import numpy as np
from jax import lax

HEAD = 128
Q_HEADS = 24
KV_HEADS = 4
FF = 8192
EXPERTS = 4
TOP = 2
MICRO = 2
MB_ROWS = 8
CACHE = 96
D = 3072
CAP = 6
TOKENS = 256
N_ATTN = 16


def draw_queries(key, part):
    key = jax.random.fold_in(key, 11)
    values = jnp.clip(jax.random.normal(key, (TOKENS, Q_HEADS * HEAD), jnp.float32), -6.0, 6.0)
    return values.astype(jnp.bfloat16)


def draw_key_cache(key, part):
    key = jax.random.fold_in(key, 13)
    values = jnp.clip(jax.random.normal(key, (TOKENS, CACHE, KV_HEADS * HEAD), jnp.float32), -6.0, 6.0)
    return values.astype(jnp.bfloat16)


def draw_new_keys(key, part):
    key = jax.random.fold_in(key, 15)
    values = jnp.clip(jax.random.normal(key, (TOKENS, KV_HEADS * HEAD), jnp.float32), -6.0, 6.0)
    return values.astype(jnp.bfloat16)


def draw_residual(key, part):
    key = jax.random.fold_in(key, 17)
    base_key = jax.random.fold_in(key, 2)
    values = jnp.clip(jax.random.normal(base_key, (TOKENS, Q_HEADS * HEAD), jnp.float32), -6.0, 6.0)
    return values.astype(jnp.bfloat16)


def place_ends(array, stream_key, least, top_value):
    shape = array.shape
    index_at = [jax.random.randint(jax.random.fold_in(stream_key, axis), (), 0, shape[axis]) for axis in range(len(shape))]
    array = array.at[tuple(index_at)].set(least)
    longest = shape.index(max(shape))
    index_at[longest] = (index_at[longest] + 1) % shape[longest]
    return array.at[tuple(index_at)].set(top_value)


def levels(stream_key, dims, cuts, least, top_value):
    factor_of, own = 1.0, jax.random.fold_in(stream_key, 6)
    for axis_at, blocks in cuts:
        steps = jnp.exp(jax.random.uniform(jax.random.fold_in(own, axis_at), (blocks,), jnp.float32, least / len(cuts), top_value / len(cuts)))
        factor_of = factor_of * jnp.repeat(steps, dims[axis_at] // blocks).reshape([-1 if axis == axis_at else 1 for axis in range(len(dims))])
    return factor_of


def profile(count, total, bound, slope):
    portions = [(1 << 20) // math.isqrt(rank ** slope) + 1 for rank in range(2, count + 1)]
    spare, holding = total - bound - (count - 1), [1] * (count - 1)
    while spare > 0:
        free = [i for i in range(count - 1) if holding[i] < bound]
        mass, budget = sum([portions[i] for i in free]), spare
        for i in free:
            addition = min(bound - holding[i], max(1, budget * portions[i] // mass), spare)
            holding[i] = holding[i] + addition
            spare = spare - addition
    return np.array([bound] + holding)


def uneven_parts(stream_key, number_of, total, reach, lean):
    if number_of == 2:
        one = jax.random.randint(stream_key, (), max(1, total - reach), min(reach, total - 1) + 1)
        return jnp.stack([one, total - one])
    tallies = jnp.asarray(profile(number_of, total, reach, lean), jnp.int32)
    twos = (number_of - 1) // 2
    donor, receiver = tallies[1:1 + 2 * twos:2], tallies[2:2 + 2 * twos:2]
    room = jnp.minimum(donor - 1, reach - receiver)
    shifted = jax.random.randint(jax.random.fold_in(stream_key, 1), (twos,), 0, 1 << 20) % (room + 1)
    tallies = tallies.at[1:1 + 2 * twos:2].set(donor - shifted).at[2:2 + 2 * twos:2].set(receiver + shifted)
    return tallies[jax.random.permutation(jax.random.fold_in(stream_key, 2), number_of)]


def routed_block(key, own, number, rows, number_of, top, reach, lean):
    order = jax.random.permutation(key, number_of)
    packed, usual = shares(number_of, rows * top, reach, lean, True), shares(number_of, rows * top, reach, lean, False)
    places = jnp.arange(number_of)

    def named(sizes, rotation):
        used = int((sizes > 0).sum())
        fixed = max(1, used // 4)
        shifted = fixed + (places - fixed + rotation * (used - fixed)) % max(1, number_of - fixed)
        return jnp.zeros((number_of,), jnp.int32).at[order[jnp.where(places < fixed, places, shifted)]].set(jnp.asarray(sizes, jnp.int32))

    sizes = jnp.where(number % 4 == 0, named(packed, number // 4), named(usual, number - number // 4 - 1))
    mixed = jax.random.permutation(jax.random.fold_in(own, 3), number_of)
    giver, receiver = mixed[0:number_of // 2 * 2:2], mixed[1:number_of // 2 * 2:2]
    margin = jnp.minimum(sizes[giver] - 1, reach - sizes[receiver]) // 2
    margin = jnp.where((giver == order[0]) | (receiver == order[0]) | (sizes[receiver] == 0), 0, jnp.maximum(margin, 0))
    shifted = jax.random.randint(jax.random.fold_in(own, 4), (number_of // 2,), 0, 1 << 20) % (margin + 1)
    sizes = sizes.at[giver].add(-shifted).at[receiver].add(shifted)
    items = jnp.searchsorted(jnp.cumsum(sizes), jnp.arange(rows * top), side="right").astype(jnp.int32)
    grid = items.reshape(top, rows).T
    grid = grid[jax.random.permutation(jax.random.fold_in(own, 1), rows)]
    rotation = jax.random.randint(jax.random.fold_in(own, 2), (rows, 1), 0, top)
    return jnp.take_along_axis(grid, (jnp.arange(top)[None, :] + rotation) % top, axis=1)


def shares(number_of, total, most, skew, full):
    weights = [(1 << 20) // math.isqrt(rank ** skew) + 1 for rank in range(1, number_of + 1)]
    largest = most if full else min(most, max(-(-total // number_of), total * weights[0] // sum(weights)))
    least = 1 if total - largest >= number_of - 1 else 0
    holding, spare = [largest] + [least] * (number_of - 1), total - largest - least * (number_of - 1)
    while spare > 0:
        free = [i for i in range(1, number_of) if holding[i] < largest] or [i for i in range(1, number_of) if holding[i] < most]
        whole, remaining = sum([weights[i] for i in free]), spare
        for i in free:
            addition = min(most - holding[i], max(1, remaining * weights[i] // whole), spare)
            holding[i] = holding[i] + addition
            spare = spare - addition
    return np.array(holding)


def gaussian(key, shape, spread, most, shards=(), held_as=jnp.bfloat16):
    result = jax.random.normal(key, shape, jnp.float32) * spread
    if len(shards) > 0:
        result = levels(key, shape, shards, -0.22, 0.18) * result
    return jnp.clip(result, min=-most, max=most).astype(held_as)


def setup_inputs(seed: int = 0, part: int = 0) -> dict:
    keys = jax.random.split(jax.random.key(seed), 14)
    part_splits = jax.random.split(jax.random.fold_in(keys[13], part), 14)
    queries = draw_queries(jax.random.fold_in(jax.random.fold_in(keys[13], part), 71), part)
    residual = draw_residual(jax.random.fold_in(jax.random.fold_in(keys[13], part), 71), part)
    key_cache = draw_key_cache(jax.random.fold_in(jax.random.fold_in(keys[13], part), 71), part)
    value_cache = gaussian(part_splits[3], (TOKENS, CACHE, KV_HEADS * HEAD), 1.0, 6.0, ((0, 16),))
    new_keys = draw_new_keys(jax.random.fold_in(jax.random.fold_in(keys[13], part), 71), part)
    new_values = gaussian(part_splits[5], (TOKENS, KV_HEADS * HEAD), 1.0, 6.0, ((0, 16),))
    cache_len = uneven_parts(part_splits[6], TOKENS, TOKENS * CACHE // 2, CACHE, 2).astype(jnp.int32)
    norm_gain = jnp.clip(1.0 + 0.1 * jax.random.normal(keys[7], (D,), jnp.float32), 0.5, 1.5)
    expert_ids_keys = jax.random.split(jax.random.fold_in(part_splits[8], 1), TOKENS // MB_ROWS)
    expert_ids_turns = jax.random.permutation(jax.random.fold_in(part_splits[8], 3), TOKENS // MB_ROWS)
    expert_ids = jax.vmap(lambda own, number: routed_block(jax.random.fold_in(part_splits[8], 2), own, number, MB_ROWS, EXPERTS, TOP, CAP, 2))(expert_ids_keys, expert_ids_turns).reshape((TOKENS, TOP))
    gate_fixed = place_ends(jax.random.randint(part_splits[9], (TOKENS, TOP), 1, 4097), jax.random.fold_in(part_splits[9], 1), 1, 4096).astype(jnp.int32)
    gate_weight = gaussian(keys[10], (D, EXPERTS * FF), D ** -0.5, 0.109375, ((1, 16),))
    up_weight = gaussian(keys[11], (D, EXPERTS * FF), D ** -0.5, 0.109375, ((1, 16),))
    down_weight = gaussian(keys[12], (EXPERTS * FF, D), FF ** -0.5, 0.0625, ((0, 16),))
    return {"queries": queries, "residual": residual, "key_cache": key_cache, "value_cache": value_cache, "new_keys": new_keys, "new_values": new_values, "cache_len": cache_len, "norm_gain": norm_gain, "expert_ids": expert_ids, "gate_fixed": gate_fixed, "gate_weight": gate_weight, "up_weight": up_weight, "down_weight": down_weight}


EPS = 1e-05
FIXED_ONE = 4096.0

def attend(queries, residual, key_cache, value_cache, new_keys, new_values, cache_len):
    rows_all = queries.shape[0]
    grouped = Q_HEADS // KV_HEADS
    query_heads = queries.astype(jnp.float32).reshape(rows_all, KV_HEADS, grouped, HEAD)
    key_heads = key_cache.astype(jnp.float32).reshape(rows_all, CACHE, KV_HEADS, HEAD)
    value_heads = value_cache.astype(jnp.float32).reshape(rows_all, CACHE, KV_HEADS, HEAD)
    own_key = new_keys.astype(jnp.float32).reshape(rows_all, KV_HEADS, HEAD)
    own_value = new_values.astype(jnp.float32).reshape(rows_all, KV_HEADS, HEAD)
    scaling = 1.0 / math.sqrt(HEAD)
    scores = jnp.einsum('tkgh,tpkh->tkgp', query_heads, key_heads) * scaling
    live_mask = jnp.arange(CACHE)[None, :] < cache_len[:, None]
    scores = jnp.where(live_mask[:, None, None, :], scores, -jnp.inf)
    own_score = jnp.einsum('tkgh,tkh->tkg', query_heads, own_key) * scaling
    highest = jnp.maximum(lax.optimization_barrier(jnp.max(scores, axis=-1)), own_score)
    exponent = jnp.exp(scores - highest[..., None])
    own_weight = jnp.exp(own_score - highest)
    totals = lax.optimization_barrier(jnp.sum(exponent, axis=-1)) + own_weight
    probabilities = lax.optimization_barrier((exponent / totals[..., None]).astype(jnp.bfloat16)).astype(jnp.float32)
    own_prob = lax.optimization_barrier((own_weight / totals).astype(jnp.bfloat16)).astype(jnp.float32)
    attended = jnp.einsum('tkgp,tpkh->tkgh', probabilities, value_heads)
    attended = attended + own_prob[..., None] * own_value[:, :, None, :]
    attended = attended.reshape(rows_all, Q_HEADS * HEAD)
    return (residual.astype(jnp.float32) + attended).astype(jnp.bfloat16)

def expert_rows(gathered, gate_cols, up_cols, down_rows):
    gate_act = jnp.dot(gathered, gate_cols, preferred_element_type=jnp.float32)
    up_act = jnp.dot(gathered, up_cols, preferred_element_type=jnp.float32)
    activated = (jax.nn.silu(gate_act) * up_act).astype(jnp.bfloat16)
    splits = N_ATTN // EXPERTS
    shard_width = FF // splits
    summed = jnp.zeros((gathered.shape[0], down_rows.shape[1]), jnp.float32)
    for shard in range(splits):
        lower = shard * shard_width
        partial_value = jnp.dot(activated[:, lower:lower + shard_width], down_rows[lower:lower + shard_width], preferred_element_type=jnp.float32).astype(jnp.bfloat16)
        summed = summed + lax.optimization_barrier(partial_value).astype(jnp.float32)
    return summed

def reference(queries, residual, key_cache, value_cache, new_keys, new_values, cache_len, norm_gain, expert_ids, gate_fixed, gate_weight, up_weight, down_weight):
    hidden = attend(queries, residual, key_cache, value_cache, new_keys, new_values, cache_len)
    hidden_f = lax.optimization_barrier(hidden).astype(jnp.float32)
    mean_square = lax.optimization_barrier(jnp.mean(hidden_f * hidden_f, axis=-1, keepdims=True))
    normed = (hidden_f * lax.rsqrt(mean_square + EPS) * norm_gain[None, :]).astype(jnp.bfloat16)
    flattened = expert_ids.reshape(-1)
    owners = (jnp.arange(flattened.shape[0]) // TOP).astype(jnp.int32)
    gate_flat = gate_fixed.reshape(-1).astype(jnp.float32) / FIXED_ONE
    limit = N_ATTN * MICRO * CAP
    mixture = jnp.zeros(hidden_f.shape, jnp.float32)
    for expert in range(EXPERTS):
        matches = flattened == expert
        ranking = jnp.cumsum(matches.astype(jnp.int32)) - 1
        placing = jnp.where(matches, ranking, limit).astype(jnp.int32)
        row_index = jnp.zeros((limit + 1,), jnp.int32).at[placing].set(owners)[:limit]
        row_weight = jnp.zeros((limit + 1,), jnp.float32).at[placing].set(gate_flat)[:limit]
        gathered = normed[row_index]
        lower = expert * FF
        produced = expert_rows(gathered, gate_weight[:, lower:lower + FF], up_weight[:, lower:lower + FF], down_weight[lower:lower + FF])
        mixture = mixture.at[row_index].add(row_weight[:, None] * produced)
    return (hidden_f + mixture).astype(jnp.bfloat16)
```

```python
import functools
import math

import jax
import jax.numpy as jnp
import numpy as np
from jax import lax
from jax.experimental import pallas as pl
from jax.experimental.pallas import tpu as pltpu
from jax.sharding import PartitionSpec as P

HEAD = 128
Q_HEADS = 24
KV_HEADS = 4
EXPERTS = 4
TOP = 2
MB_ROWS = 8
CACHE = 96
CAP = 6
EPS = 1e-05
FEAT = 4
ROWS = 16
SLOTS = CAP * ROWS // MB_ROWS
PACK = FEAT * SLOTS
GROUP = Q_HEADS // KV_HEADS
LANES = FEAT * ROWS
MIB = 2**20
BF16, F32, I32 = jnp.bfloat16, jnp.float32, jnp.int32


def iota(shape, dim):
    return lax.broadcasted_iota(I32, shape, dim)


def slots_of(plane, ids_ref):
    expert = (plane + iota((8, ROWS), 0)) & (EXPERTS - 1)
    first = ids_ref[0:1, :] == expert
    second = ids_ref[1:2, :] == expert
    named = jnp.where(first | second, 1.0, 0.0).astype(BF16)
    token, lane_token = iota((ROWS, LANES), 0), iota((ROWS, LANES), 1) & (ROWS - 1)
    spread = jnp.where(token == lane_token, 1.0, 0.0).astype(BF16)
    earlier = (token < lane_token) & ((token >> 3) == (lane_token >> 3))
    earlier = jnp.where(earlier, 1.0, 0.0).astype(BF16)
    named_wide = jnp.dot(named, spread, preferred_element_type=F32)
    rank = jnp.dot(named, earlier, preferred_element_type=F32).astype(I32)
    batch = (iota((8, LANES), 1) & (ROWS - 1)) >> 3
    slot = jnp.where(named_wide > 0.5, batch * CAP + rank, -1)
    return slot, spread, first, second


def matching(slot, s):
    row, lane = iota((PACK, LANES), 0), iota((PACK, LANES), 1)
    chunk = sum((row >= SLOTS * f).astype(I32) for f in range(1, FEAT))
    return (chunk == (lane >> 4)) & (slot[s : s + 1, :] == row - SLOTS * chunk)


def attention_kernel(
    plane_ref, len_ref, q_ref, res_ref, k_hbm, v_hbm, nk_ref, nv_ref, gain_ref, ids_ref,
    hid_ref, b0_ref, b1_ref, b2_ref, b3_ref,
    k_ref, v_ref, q_scr, o_scr, sems,
):
    parts = sems.shape[1]
    step = ROWS // parts
    copies = []
    for c in range(parts):
        own = pl.ds(c * step, step)
        pair = (
            pltpu.make_async_copy(k_hbm.at[own], k_ref.at[own], sems.at[0, c]),
            pltpu.make_async_copy(v_hbm.at[own], v_ref.at[own], sems.at[1, c]),
        )
        for copy in pair:
            copy.start()
        copies.append(pair)
    for h in range(Q_HEADS):
        q_scr[pl.ds(h, ROWS, stride=Q_HEADS), :] = q_ref[:, h * HEAD : (h + 1) * HEAD].astype(F32)
    row, col = iota((Q_HEADS, KV_HEADS * HEAD), 0), iota((Q_HEADS, KV_HEADS * HEAD), 1)
    reads = sum((row >= GROUP * k).astype(I32) for k in range(1, KV_HEADS)) == (col >> 7)
    head_row = iota((Q_HEADS, HEAD), 0)
    position, own_col = iota((Q_HEADS, CACHE), 1), iota((Q_HEADS, ROWS), 1)
    scaling = 1.0 / math.sqrt(HEAD)
    contract = (((1,), (1,)), ((), ()))
    nk, nv = nk_ref[...], nv_ref[...]
    low = -1e30
    for t in range(ROWS):
        if t % step == 0:
            for copy in copies[t // step]:
                copy.wait()
        q = q_scr[t * Q_HEADS : (t + 1) * Q_HEADS, :]
        q = jnp.where(reads, jnp.concatenate([q] * KV_HEADS, axis=1), 0.0).astype(BF16)
        s1 = lax.dot_general(q, k_ref[t], contract, preferred_element_type=F32) * scaling
        s2 = lax.dot_general(q, nk, contract, preferred_element_type=F32) * scaling
        s1 = jnp.where(position < len_ref[t], s1, low)
        s2 = jnp.where(own_col == t, s2, low)
        top = jnp.maximum(jnp.max(s1, axis=1, keepdims=True), jnp.max(s2, axis=1, keepdims=True))
        e1, e2 = jnp.exp(s1 - top), jnp.exp(s2 - top)
        total = jnp.sum(e1, axis=1, keepdims=True) + jnp.sum(e2, axis=1, keepdims=True)
        p1, p2 = (e1 / total).astype(BF16), (e2 / total).astype(BF16)
        o = jnp.dot(p1, v_ref[t], preferred_element_type=F32)
        o = o + jnp.dot(p2, nv, preferred_element_type=F32)
        picked = o[:, 0:HEAD]
        for k in range(1, KV_HEADS):
            picked = jnp.where(head_row >= GROUP * k, o[:, k * HEAD : (k + 1) * HEAD], picked)
        o_scr[t * Q_HEADS : (t + 1) * Q_HEADS, :] = picked
    squares = jnp.zeros((ROWS, HEAD), F32)
    hidden = []
    for h in range(Q_HEADS):
        span = slice(h * HEAD, (h + 1) * HEAD)
        part = (res_ref[:, span].astype(F32) + o_scr[pl.ds(h, ROWS, stride=Q_HEADS), :]).astype(BF16)
        hid_ref[:, span] = part
        part = part.astype(F32)
        squares = squares + part * part
        hidden.append(part)
    width = Q_HEADS * HEAD
    scale = lax.rsqrt(jnp.sum(squares, axis=1, keepdims=True) * (1.0 / width) + EPS)
    per = Q_HEADS // FEAT
    chunks = []
    for f in range(FEAT):
        heads = [
            (hidden[h] * scale * gain_ref[:, h * HEAD : (h + 1) * HEAD]).astype(BF16)
            for h in range(f * per, (f + 1) * per)
        ]
        chunks.append(jnp.concatenate(heads, axis=1))
    stacked = jnp.concatenate(chunks, axis=0)
    slot, _, _, _ = slots_of(plane_ref[0], ids_ref)
    for s, out in enumerate((b0_ref, b1_ref, b2_ref, b3_ref)):
        picker = jnp.where(matching(slot, s), 1.0, 0.0).astype(BF16)
        out[...] = jnp.dot(picker, stacked, preferred_element_type=F32).astype(BF16)


def blend_kernel(plane_ref, ids_ref, gate_ref, out_ref):
    slot, spread, first, second = slots_of(plane_ref[0], ids_ref)
    gate = jnp.where(first, gate_ref[0:1, :], 0) + jnp.where(second, gate_ref[1:2, :], 0)
    high = jnp.dot((gate >> 6).astype(F32).astype(BF16), spread, preferred_element_type=F32)
    rest = jnp.dot((gate & 63).astype(F32).astype(BF16), spread, preferred_element_type=F32)
    for s in range(EXPERTS):
        match = matching(slot, s)
        rows = slice(s * PACK, (s + 1) * PACK)
        out_ref[rows, 0:LANES] = jnp.where(match, high[s : s + 1, :], 0.0).astype(BF16)
        out_ref[rows, LANES : 2 * LANES] = jnp.where(match, rest[s : s + 1, :], 0.0).astype(BF16)


def experts_kernel(slabs, *refs):
    blocks = refs[: slabs * EXPERTS]
    order_ref, back_ref, gate_ref, up_ref, down_ref = refs[slabs * EXPERTS : slabs * EXPERTS + 5]
    outs = refs[slabs * EXPERTS + 5 : -3]
    x_ref, a_ref, y_ref = refs[-3:]
    rows = EXPERTS * SLOTS
    part = y_ref.shape[2]
    order = order_ref[...]
    for q in range(slabs):
        packed = jnp.concatenate([b[...] for b in blocks[q * EXPERTS : (q + 1) * EXPERTS]], axis=0)
        x = jnp.dot(order, packed, preferred_element_type=F32).astype(BF16)
        for f in range(FEAT):
            x_ref[q * rows : (q + 1) * rows, f * part : (f + 1) * part] = x[f * rows : (f + 1) * rows]
    x = x_ref[...]
    units = gate_ref.shape[1]
    tile = min(512, units)
    for j in range(units // tile):
        span = slice(j * tile, (j + 1) * tile)
        g = jnp.dot(x, gate_ref[:, span], preferred_element_type=F32)
        u = jnp.dot(x, up_ref[:, span], preferred_element_type=F32)
        a_ref[:, span] = (g / (1.0 + jnp.exp(-g)) * u).astype(BF16)
    a = a_ref[...]
    for f in range(FEAT):
        span = slice(f * part, (f + 1) * part)
        y_ref[f] = jnp.dot(a, down_ref[:, span], preferred_element_type=F32).astype(BF16)
    back = back_ref[...]
    for q in range(slabs):
        stacked = jnp.concatenate([y_ref[f, q * rows : (q + 1) * rows, :] for f in range(FEAT)], axis=0)
        packed = jnp.dot(back, stacked, preferred_element_type=F32).astype(BF16)
        half = q // (slabs // 2)
        at = (q % (slabs // 2)) * EXPERTS * PACK
        outs[half][at : at + EXPERTS * PACK, :] = packed


def mix_kernel(hid_ref, blend_ref, m0_ref, m1_ref, m2_ref, m3_ref, out_ref):
    part = m0_ref.shape[1]
    packed = jnp.concatenate([m0_ref[...], m1_ref[...], m2_ref[...], m3_ref[...]], axis=0)
    mixed = lax.dot_general(blend_ref[...], packed, (((0,), (0,)), ((), ())), preferred_element_type=F32)
    mixed = mixed[:LANES] * (1.0 / 64.0) + mixed[LANES:] * (1.0 / 4096.0)
    for f in range(FEAT):
        span = slice(f * part, (f + 1) * part)
        own = hid_ref[:, span].astype(F32) + mixed[f * ROWS : (f + 1) * ROWS]
        out_ref[:, span] = own.astype(BF16)


VMEM = pl.BlockSpec(memory_space=pltpu.VMEM)
SMEM = pl.BlockSpec(memory_space=pltpu.SMEM)
HBM = pl.BlockSpec(memory_space=pl.ANY)


def params(mib):
    return pltpu.CompilerParams(vmem_limit_bytes=mib * MIB)


def local(
    queries, residual, key_cache, value_cache, new_keys, new_values, cache_len, norm_gain,
    expert_ids, gate_fixed, gate_weight, up_weight, down_weight,
):
    devices = lax.axis_size("attn")
    splits = devices // EXPERTS
    width = queries.shape[1]
    part = width // FEAT
    kv_width = key_cache.shape[2]
    plane = (lax.axis_index("attn") // splits).astype(I32).reshape(1)
    ids, gates = expert_ids.T, gate_fixed.T
    block = jax.ShapeDtypeStruct((PACK, part), BF16)

    hidden, *blocks = pl.pallas_call(
        attention_kernel,
        out_shape=[jax.ShapeDtypeStruct((ROWS, width), BF16)] + [block] * EXPERTS,
        in_specs=[SMEM, SMEM, VMEM, VMEM, HBM, HBM, VMEM, VMEM, VMEM, VMEM],
        out_specs=[VMEM] * (1 + EXPERTS),
        scratch_shapes=[
            pltpu.VMEM((ROWS, CACHE, kv_width), BF16),
            pltpu.VMEM((ROWS, CACHE, kv_width), BF16),
            pltpu.VMEM((ROWS * Q_HEADS, HEAD), F32),
            pltpu.VMEM((ROWS * Q_HEADS, HEAD), F32),
            pltpu.SemaphoreType.DMA((2, 4)),
        ],
        compiler_params=params(14),
        cost_estimate=pl.CostEstimate(flops=10**9, bytes_accessed=20 * 10**6, transcendentals=0),
        name="attention",
    )(
        plane, cache_len, queries, residual, key_cache, value_cache, new_keys, new_values,
        norm_gain.reshape(1, width), ids,
    )
    blend = pl.pallas_call(
        blend_kernel,
        out_shape=jax.ShapeDtypeStruct((EXPERTS * PACK, 2 * LANES), BF16),
        in_specs=[SMEM, VMEM, VMEM],
        out_specs=VMEM,
        compiler_params=params(4),
        name="blend",
    )(plane, ids, gates)

    def shifted(x, s):
        return lax.ppermute(x, "attn", [(i, (i + s * splits) % devices) for i in range(devices)])

    def swapped(x, bit):
        return lax.ppermute(x, "attn", [(i, i ^ bit) for i in range(devices)])

    got = [blocks[0]] + [shifted(blocks[s], s) for s in range(1, EXPERTS)]
    bit = splits // 2
    while bit >= 1:
        got = got + [swapped(b, bit) for b in got]
        bit //= 2
    total = splits * EXPERTS * SLOTS
    to = np.arange(EXPERTS * PACK)
    f, s, j = to // (EXPERTS * SLOTS), to // SLOTS % EXPERTS, to % SLOTS
    order = np.zeros((EXPERTS * PACK, EXPERTS * PACK), np.float32)
    order[to, s * PACK + f * SLOTS + j] = 1.0
    weights = [pltpu.with_memory_space_constraint(w, pltpu.VMEM) for w in (gate_weight, up_weight, down_weight)]
    units = gate_weight.shape[1]
    keep, send = pl.pallas_call(
        functools.partial(experts_kernel, splits),
        out_shape=[jax.ShapeDtypeStruct((splits // 2 * EXPERTS * PACK, part), BF16)] * 2,
        in_specs=[VMEM] * (splits * EXPERTS + 5),
        out_specs=[VMEM] * 2,
        scratch_shapes=[
            pltpu.VMEM((total, width), BF16),
            pltpu.VMEM((total, units), BF16),
            pltpu.VMEM((FEAT, total, part), BF16),
        ],
        compiler_params=params(16 if total <= 192 else 36),
        cost_estimate=pl.CostEstimate(
            flops=6 * total * width * units, bytes_accessed=6 * width * units, transcendentals=0
        ),
        name="experts",
    )(*got, jnp.asarray(order, BF16), jnp.asarray(order.T, BF16), *weights)

    def plus(a, b):
        return (a.astype(F32) + b.astype(F32)).astype(BF16)

    keep = plus(keep, swapped(send, 1))
    rows, bit = keep.shape[0], 2
    while rows > EXPERTS * PACK * 2:
        keep = plus(keep[: rows // 2], swapped(keep[rows // 2 :], bit))
        rows, bit = rows // 2, bit * 2
    summed = [
        plus(keep[s * PACK : (s + 1) * PACK], swapped(keep[rows // 2 + s * PACK : rows // 2 + (s + 1) * PACK], bit))
        for s in range(EXPERTS)
    ]
    mine = [summed[0]] + [shifted(summed[s], -s) for s in range(1, EXPERTS)]
    return pl.pallas_call(
        mix_kernel,
        out_shape=jax.ShapeDtypeStruct((ROWS, width), BF16),
        in_specs=[VMEM] * (2 + EXPERTS),
        out_specs=VMEM,
        compiler_params=params(8),
        name="mix",
    )(hidden, blend, *mine)


def solution(mesh):
    rows = P(("groups", "attn"), None)
    cached = P(("groups", "attn"), None, None)
    in_specs = (
        rows, rows, cached, cached, rows, rows, P(("groups", "attn")), P(), rows, rows,
        P(None, "attn"), P(None, "attn"), P("attn", None),
    )
    return jax.shard_map(local, mesh=mesh, in_specs=in_specs, out_specs=rows, check_vma=False)
```

```python
import functools
import math

import jax
import jax.numpy as jnp
import numpy as np
from jax import lax
from jax.experimental import pallas as pl
from jax.experimental.pallas import tpu as pltpu
from jax.sharding import PartitionSpec as P

HEAD = 128
Q_HEADS = 24
KV_HEADS = 4
EXPERTS = 4
TOP = 2
MB_ROWS = 8
CACHE = 96
CAP = 6
EPS = 1e-05
FEAT = 4
ROWS = 16
SLOTS = CAP * ROWS // MB_ROWS
PACK = FEAT * SLOTS
GROUP = Q_HEADS // KV_HEADS
LANES = FEAT * ROWS
MIB = 2**20
BF16, F32, I32 = jnp.bfloat16, jnp.float32, jnp.int32


def iota(shape, dim):
    return lax.broadcasted_iota(I32, shape, dim)


def slots_of(plane, ids_ref):
    expert = (plane + iota((8, ROWS), 0)) & (EXPERTS - 1)
    first = ids_ref[0:1, :] == expert
    second = ids_ref[1:2, :] == expert
    named = jnp.where(first | second, 1.0, 0.0).astype(BF16)
    token, lane_token = iota((ROWS, LANES), 0), iota((ROWS, LANES), 1) & (ROWS - 1)
    spread = jnp.where(token == lane_token, 1.0, 0.0).astype(BF16)
    earlier = (token < lane_token) & ((token >> 3) == (lane_token >> 3))
    earlier = jnp.where(earlier, 1.0, 0.0).astype(BF16)
    named_wide = jnp.dot(named, spread, preferred_element_type=F32)
    rank = jnp.dot(named, earlier, preferred_element_type=F32).astype(I32)
    batch = (iota((8, LANES), 1) & (ROWS - 1)) >> 3
    slot = jnp.where(named_wide > 0.5, batch * CAP + rank, -1)
    return slot, spread, first, second


def matching(slot, s):
    row, lane = iota((PACK, LANES), 0), iota((PACK, LANES), 1)
    chunk = sum((row >= SLOTS * f).astype(I32) for f in range(1, FEAT))
    return (chunk == (lane >> 4)) & (slot[s : s + 1, :] == row - SLOTS * chunk)


def attention_kernel(
    plane_ref, *refs
):
    operands, outs, scratch = refs[:9], refs[9:14], refs[14:]
    len_hbm, q_hbm, res_hbm, k_hbm, v_hbm, nk_hbm, nv_hbm, gain_hbm, ids_hbm = operands
    hid_ref, *block_refs = outs
    len_ref, q_ref, res_ref, k_ref, v_ref, nk_ref, nv_ref, gain_ref, ids_ref, q_scr, o_scr, sems, small = scratch
    parts = sems.shape[1]
    step = ROWS // parts

    def fetch(source, target, sem):
        copy = pltpu.make_async_copy(source, target, sem)
        copy.start()
        return copy

    early = [
        fetch(q_hbm, q_ref, small.at[0]),
        fetch(nk_hbm, nk_ref, small.at[1]),
        fetch(nv_hbm, nv_ref, small.at[2]),
        fetch(len_hbm, len_ref, small.at[3]),
    ]
    copies = []
    for c in range(parts):
        own = pl.ds(c * step, step)
        copies.append((
            fetch(k_hbm.at[own], k_ref.at[own], sems.at[0, c]),
            fetch(v_hbm.at[own], v_ref.at[own], sems.at[1, c]),
        ))
    late = [
        fetch(res_hbm, res_ref, small.at[4]),
        fetch(gain_hbm, gain_ref, small.at[5]),
        fetch(ids_hbm, ids_ref, small.at[6]),
    ]
    for copy in early:
        copy.wait()
    for h in range(Q_HEADS):
        q_scr[pl.ds(h, ROWS, stride=Q_HEADS), :] = q_ref[:, h * HEAD : (h + 1) * HEAD].astype(F32)
    row, col = iota((Q_HEADS, KV_HEADS * HEAD), 0), iota((Q_HEADS, KV_HEADS * HEAD), 1)
    reads = sum((row >= GROUP * k).astype(I32) for k in range(1, KV_HEADS)) == (col >> 7)
    head_row = iota((Q_HEADS, HEAD), 0)
    position, own_col = iota((Q_HEADS, CACHE), 1), iota((Q_HEADS, ROWS), 1)
    scaling = 1.0 / math.sqrt(HEAD)
    contract = (((1,), (1,)), ((), ()))
    nk, nv = nk_ref[...], nv_ref[...]
    low = -1e30
    for t in range(ROWS):
        if t % step == 0:
            for copy in copies[t // step]:
                copy.wait()
        q = q_scr[t * Q_HEADS : (t + 1) * Q_HEADS, :]
        q = jnp.where(reads, jnp.concatenate([q] * KV_HEADS, axis=1), 0.0).astype(BF16)
        s1 = lax.dot_general(q, k_ref[t], contract, preferred_element_type=F32) * scaling
        s2 = lax.dot_general(q, nk, contract, preferred_element_type=F32) * scaling
        s1 = jnp.where(position < len_ref[t], s1, low)
        s2 = jnp.where(own_col == t, s2, low)
        top = jnp.maximum(jnp.max(s1, axis=1, keepdims=True), jnp.max(s2, axis=1, keepdims=True))
        e1, e2 = jnp.exp(s1 - top), jnp.exp(s2 - top)
        total = jnp.sum(e1, axis=1, keepdims=True) + jnp.sum(e2, axis=1, keepdims=True)
        p1, p2 = (e1 / total).astype(BF16), (e2 / total).astype(BF16)
        o = jnp.dot(p1, v_ref[t], preferred_element_type=F32)
        o = o + jnp.dot(p2, nv, preferred_element_type=F32)
        picked = o[:, 0:HEAD]
        for k in range(1, KV_HEADS):
            picked = jnp.where(head_row >= GROUP * k, o[:, k * HEAD : (k + 1) * HEAD], picked)
        o_scr[t * Q_HEADS : (t + 1) * Q_HEADS, :] = picked
    for copy in late:
        copy.wait()
    squares = jnp.zeros((ROWS, HEAD), F32)
    hidden = []
    for h in range(Q_HEADS):
        span = slice(h * HEAD, (h + 1) * HEAD)
        part = (res_ref[:, span].astype(F32) + o_scr[pl.ds(h, ROWS, stride=Q_HEADS), :]).astype(BF16)
        hid_ref[:, span] = part
        part = part.astype(F32)
        squares = squares + part * part
        hidden.append(part)
    width = Q_HEADS * HEAD
    scale = lax.rsqrt(jnp.sum(squares, axis=1, keepdims=True) * (1.0 / width) + EPS)
    per = Q_HEADS // FEAT
    chunks = []
    for f in range(FEAT):
        heads = [
            (hidden[h] * scale * gain_ref[:, h * HEAD : (h + 1) * HEAD]).astype(BF16)
            for h in range(f * per, (f + 1) * per)
        ]
        chunks.append(jnp.concatenate(heads, axis=1))
    stacked = jnp.concatenate(chunks, axis=0)
    slot, _, _, _ = slots_of(plane_ref[0], ids_ref)
    for s, out in enumerate(block_refs):
        picker = jnp.where(matching(slot, s), 1.0, 0.0).astype(BF16)
        out[...] = jnp.dot(picker, stacked, preferred_element_type=F32).astype(BF16)


def blend_kernel(plane_ref, ids_ref, gate_ref, out_ref):
    slot, spread, first, second = slots_of(plane_ref[0], ids_ref)
    gate = jnp.where(first, gate_ref[0:1, :], 0) + jnp.where(second, gate_ref[1:2, :], 0)
    high = jnp.dot((gate >> 6).astype(F32).astype(BF16), spread, preferred_element_type=F32)
    rest = jnp.dot((gate & 63).astype(F32).astype(BF16), spread, preferred_element_type=F32)
    for s in range(EXPERTS):
        match = matching(slot, s)
        rows = slice(s * PACK, (s + 1) * PACK)
        out_ref[rows, 0:LANES] = jnp.where(match, high[s : s + 1, :], 0.0).astype(BF16)
        out_ref[rows, LANES : 2 * LANES] = jnp.where(match, rest[s : s + 1, :], 0.0).astype(BF16)


def experts_kernel(slabs, *refs):
    blocks = refs[: slabs * EXPERTS]
    order_ref, back_ref, gate_ref, up_ref, down_ref = refs[slabs * EXPERTS : slabs * EXPERTS + 5]
    outs = refs[slabs * EXPERTS + 5 : -3]
    x_ref, a_ref, y_ref = refs[-3:]
    rows = EXPERTS * SLOTS
    part = y_ref.shape[2]
    order = order_ref[...]
    for q in range(slabs):
        packed = jnp.concatenate([b[...] for b in blocks[q * EXPERTS : (q + 1) * EXPERTS]], axis=0)
        x = jnp.dot(order, packed, preferred_element_type=F32).astype(BF16)
        for f in range(FEAT):
            x_ref[q * rows : (q + 1) * rows, f * part : (f + 1) * part] = x[f * rows : (f + 1) * rows]
    x = x_ref[...]
    units = gate_ref.shape[1]
    tile = min(512, units)
    for j in range(units // tile):
        span = slice(j * tile, (j + 1) * tile)
        g = jnp.dot(x, gate_ref[:, span], preferred_element_type=F32)
        u = jnp.dot(x, up_ref[:, span], preferred_element_type=F32)
        a_ref[:, span] = (g / (1.0 + jnp.exp(-g)) * u).astype(BF16)
    a = a_ref[...]
    for f in range(FEAT):
        span = slice(f * part, (f + 1) * part)
        y_ref[f] = jnp.dot(a, down_ref[:, span], preferred_element_type=F32).astype(BF16)
    back = back_ref[...]
    for q in range(slabs):
        stacked = jnp.concatenate([y_ref[f, q * rows : (q + 1) * rows, :] for f in range(FEAT)], axis=0)
        packed = jnp.dot(back, stacked, preferred_element_type=F32).astype(BF16)
        half = q // (slabs // 2)
        at = (q % (slabs // 2)) * EXPERTS * PACK
        outs[half][at : at + EXPERTS * PACK, :] = packed


def mix_kernel(hid_ref, blend_ref, m0_ref, m1_ref, m2_ref, m3_ref, out_ref):
    part = m0_ref.shape[1]
    packed = jnp.concatenate([m0_ref[...], m1_ref[...], m2_ref[...], m3_ref[...]], axis=0)
    mixed = lax.dot_general(blend_ref[...], packed, (((0,), (0,)), ((), ())), preferred_element_type=F32)
    mixed = mixed[:LANES] * (1.0 / 64.0) + mixed[LANES:] * (1.0 / 4096.0)
    for f in range(FEAT):
        span = slice(f * part, (f + 1) * part)
        own = hid_ref[:, span].astype(F32) + mixed[f * ROWS : (f + 1) * ROWS]
        out_ref[:, span] = own.astype(BF16)


VMEM = pl.BlockSpec(memory_space=pltpu.VMEM)
SMEM = pl.BlockSpec(memory_space=pltpu.SMEM)
HBM = pl.BlockSpec(memory_space=pltpu.HBM)


def params(mib):
    return pltpu.CompilerParams(vmem_limit_bytes=mib * MIB)


def attention(plane, *operands):
    width, kv_width = operands[1].shape[1], operands[3].shape[2]
    block = jax.ShapeDtypeStruct((PACK, width // FEAT), BF16)
    pinned = [pltpu.with_memory_space_constraint(x, pltpu.HBM) for x in operands]
    return pl.pallas_call(
        attention_kernel,
        out_shape=[jax.ShapeDtypeStruct((ROWS, width), BF16)] + [block] * EXPERTS,
        in_specs=[SMEM] + [HBM] * len(operands),
        out_specs=[VMEM] * (1 + EXPERTS),
        scratch_shapes=[pltpu.SMEM(operands[0].shape, I32)]
        + [pltpu.VMEM(x.shape, x.dtype) for x in operands[1:]]
        + [
            pltpu.VMEM((ROWS * Q_HEADS, HEAD), F32),
            pltpu.VMEM((ROWS * Q_HEADS, HEAD), F32),
            pltpu.SemaphoreType.DMA((2, 4)),
            pltpu.SemaphoreType.DMA((7,)),
        ],
        compiler_params=params(6),
        cost_estimate=pl.CostEstimate(flops=40 * 10**9, bytes_accessed=4 * 10**6, transcendentals=0),
        name="attention",
    )(plane, *pinned)


def add_kernel(at, keep_ref, came_ref, out_ref):
    rows = out_ref.shape[0]
    out_ref[...] = (keep_ref[at : at + rows, :].astype(F32) + came_ref[...].astype(F32)).astype(BF16)


def add_block(keep, came, at):
    return pl.pallas_call(
        functools.partial(add_kernel, at),
        out_shape=jax.ShapeDtypeStruct(came.shape, BF16),
        in_specs=[VMEM] * 2,
        out_specs=VMEM,
        compiler_params=params(4),
        name="add_block",
    )(keep, came)


def local(
    queries, residual, key_cache, value_cache, new_keys, new_values, cache_len, norm_gain,
    expert_ids, gate_fixed, gate_weight, up_weight, down_weight,
):
    devices = lax.axis_size("attn")
    splits = devices // EXPERTS
    width = queries.shape[1]
    part = width // FEAT
    plane = (lax.axis_index("attn") // splits).astype(I32).reshape(1)
    ids, gates = expert_ids.T, gate_fixed.T
    hidden, *blocks = attention(
        plane, cache_len, queries, residual, key_cache, value_cache, new_keys, new_values,
        norm_gain.reshape(1, width), ids,
    )
    blend = pl.pallas_call(
        blend_kernel,
        out_shape=jax.ShapeDtypeStruct((EXPERTS * PACK, 2 * LANES), BF16),
        in_specs=[SMEM, VMEM, VMEM],
        out_specs=VMEM,
        compiler_params=params(4),
        name="blend",
    )(plane, ids, gates)

    def shifted(x, s):
        return lax.ppermute(x, "attn", [(i, (i + s * splits) % devices) for i in range(devices)])

    def swapped(x, bit):
        return lax.ppermute(x, "attn", [(i, i ^ bit) for i in range(devices)])

    got = [blocks[0]] + [shifted(blocks[s], s) for s in range(1, EXPERTS)]
    bit = splits // 2
    while bit >= 1:
        got = got + [swapped(b, bit) for b in got]
        bit //= 2
    total = splits * EXPERTS * SLOTS
    to = np.arange(EXPERTS * PACK)
    f, s, j = to // (EXPERTS * SLOTS), to // SLOTS % EXPERTS, to % SLOTS
    order = np.zeros((EXPERTS * PACK, EXPERTS * PACK), np.float32)
    order[to, s * PACK + f * SLOTS + j] = 1.0
    weights = [pltpu.with_memory_space_constraint(w, pltpu.VMEM) for w in (gate_weight, up_weight, down_weight)]
    units = gate_weight.shape[1]
    keep, send = pl.pallas_call(
        functools.partial(experts_kernel, splits),
        out_shape=[jax.ShapeDtypeStruct((splits // 2 * EXPERTS * PACK, part), BF16)] * 2,
        in_specs=[VMEM] * (splits * EXPERTS + 5),
        out_specs=[VMEM] * 2,
        scratch_shapes=[
            pltpu.VMEM((total, width), BF16),
            pltpu.VMEM((total, units), BF16),
            pltpu.VMEM((FEAT, total, part), BF16),
        ],
        compiler_params=params(16 if total <= 192 else 36),
        cost_estimate=pl.CostEstimate(
            flops=6 * total * width * units, bytes_accessed=6 * width * units, transcendentals=0
        ),
        name="experts",
    )(*got, jnp.asarray(order, BF16), jnp.asarray(order.T, BF16), *weights)

    def plus(a, b):
        return (a.astype(F32) + b.astype(F32)).astype(BF16)

    keep = plus(keep, swapped(send, 1))
    rows, bit = keep.shape[0], 2
    while rows > EXPERTS * PACK * 2:
        keep = plus(keep[: rows // 2], swapped(keep[rows // 2 :], bit))
        rows, bit = rows // 2, bit * 2
    summed = [None] * EXPERTS
    came = {}
    for s in (2, 1, 3, 0):
        came[s] = swapped(keep[rows // 2 + s * PACK : rows // 2 + (s + 1) * PACK], bit)
    for s in (2, 1, 3, 0):
        summed[s] = add_block(keep, came[s], s * PACK)
    mine = [summed[0]] + [shifted(summed[s], -s) for s in range(1, EXPERTS)]
    return pl.pallas_call(
        mix_kernel,
        out_shape=jax.ShapeDtypeStruct((ROWS, width), BF16),
        in_specs=[VMEM] * (2 + EXPERTS),
        out_specs=VMEM,
        compiler_params=params(8),
        name="mix",
    )(hidden, blend, *mine)


def solution(mesh):
    rows = P(("groups", "attn"), None)
    cached = P(("groups", "attn"), None, None)
    in_specs = (
        rows, rows, cached, cached, rows, rows, P(("groups", "attn")), P(), rows, rows,
        P(None, "attn"), P(None, "attn"), P("attn", None),
    )
    return jax.shard_map(local, mesh=mesh, in_specs=in_specs, out_specs=rows, check_vma=False)
```

```python
import functools
import math

import jax
import jax.numpy as jnp
import numpy as np
from jax import lax
from jax.experimental import pallas as pl
from jax.experimental.pallas import tpu as pltpu
from jax.sharding import PartitionSpec as P

HEAD = 128
Q_HEADS = 24
KV_HEADS = 4
EXPERTS = 4
TOP = 2
MB_ROWS = 8
CACHE = 96
CAP = 6
EPS = 1e-05
FEAT = 4
ROWS = 16
SLOTS = CAP * ROWS // MB_ROWS
PACK = FEAT * SLOTS
GROUP = Q_HEADS // KV_HEADS
LANES = FEAT * ROWS
MIB = 2**20
BF16, F32, I32 = jnp.bfloat16, jnp.float32, jnp.int32


def iota(shape, dim):
    return lax.broadcasted_iota(I32, shape, dim)


def slots_of(plane, ids_ref):
    expert = (plane + iota((8, ROWS), 0)) & (EXPERTS - 1)
    first = ids_ref[0:1, :] == expert
    second = ids_ref[1:2, :] == expert
    named = jnp.where(first | second, 1.0, 0.0).astype(BF16)
    token, lane_token = iota((ROWS, LANES), 0), iota((ROWS, LANES), 1) & (ROWS - 1)
    spread = jnp.where(token == lane_token, 1.0, 0.0).astype(BF16)
    earlier = (token < lane_token) & ((token >> 3) == (lane_token >> 3))
    earlier = jnp.where(earlier, 1.0, 0.0).astype(BF16)
    named_wide = jnp.dot(named, spread, preferred_element_type=F32)
    rank = jnp.dot(named, earlier, preferred_element_type=F32).astype(I32)
    batch = (iota((8, LANES), 1) & (ROWS - 1)) >> 3
    slot = jnp.where(named_wide > 0.5, batch * CAP + rank, -1)
    return slot, spread, first, second


def matching(slot, s):
    row, lane = iota((PACK, LANES), 0), iota((PACK, LANES), 1)
    chunk = sum((row >= SLOTS * f).astype(I32) for f in range(1, FEAT))
    return (chunk == (lane >> 4)) & (slot[s : s + 1, :] == row - SLOTS * chunk)


def attention_kernel(plane_ref, *refs):
    operands, outs, scratch = refs[:9], refs[9:14], refs[14:]
    len_hbm, q_hbm, res_hbm, k_hbm, v_hbm, nk_hbm, nv_hbm, gain_hbm, ids_hbm = operands
    hid_ref, *block_refs = outs
    len_ref, q_ref, res_ref, k_ref, v_ref, nk_ref, nv_ref, gain_ref, ids_ref, q_scr, o_scr, pick_scr, sems, small = scratch
    parts = sems.shape[1]
    step = ROWS // parts

    def fetch(source, target, sem):
        copy = pltpu.make_async_copy(source, target, sem)
        copy.start()
        return copy

    early = [
        fetch(ids_hbm, ids_ref, small.at[0]),
        fetch(q_hbm, q_ref, small.at[1]),
        fetch(nk_hbm, nk_ref, small.at[2]),
        fetch(nv_hbm, nv_ref, small.at[3]),
        fetch(len_hbm, len_ref, small.at[4]),
    ]
    copies = []
    for c in range(parts):
        own = pl.ds(c * step, step)
        copies.append((
            fetch(k_hbm.at[own], k_ref.at[own, pl.ds(0, CACHE)], sems.at[0, c]),
            fetch(v_hbm.at[own], v_ref.at[own, pl.ds(0, CACHE)], sems.at[1, c]),
        ))
    late = [fetch(res_hbm, res_ref, small.at[5]), fetch(gain_hbm, gain_ref, small.at[6])]
    early[0].wait()
    slot, _, _, _ = slots_of(plane_ref[0], ids_ref)
    for s in range(EXPERTS):
        pick_scr[s * PACK : (s + 1) * PACK, :] = jnp.where(matching(slot, s), 1.0, 0.0).astype(BF16)
    early[1].wait()
    for h in range(Q_HEADS):
        q_scr[pl.ds(h, ROWS, stride=Q_HEADS), :] = q_ref[:, h * HEAD : (h + 1) * HEAD].astype(F32)
    for copy in early[2:]:
        copy.wait()
    nk, nv = nk_ref[...], nv_ref[...]
    for t in range(ROWS):
        k_ref[t, CACHE:, :] = nk
        v_ref[t, CACHE:, :] = nv
    row, col = iota((Q_HEADS, KV_HEADS * HEAD), 0), iota((Q_HEADS, KV_HEADS * HEAD), 1)
    reads = sum((row >= GROUP * k).astype(I32) for k in range(1, KV_HEADS)) == (col >> 7)
    head_row = iota((Q_HEADS, HEAD), 0)
    position = iota((Q_HEADS, CACHE + ROWS), 1)
    scaling = 1.0 / math.sqrt(HEAD)
    contract = (((1,), (1,)), ((), ()))
    for c in range(parts):
        tokens = range(c * step, (c + 1) * step)
        copies[c][0].wait()
        scores = []
        for t in tokens:
            q = q_scr[t * Q_HEADS : (t + 1) * Q_HEADS, :]
            q = jnp.where(reads, jnp.concatenate([q] * KV_HEADS, axis=1), 0.0).astype(BF16)
            score = lax.dot_general(q, k_ref[t], contract, preferred_element_type=F32) * scaling
            live = (position < len_ref[t]) | (position == CACHE + t)
            scores.append(jnp.where(live, score, -1e30))
        scores = jnp.concatenate(scores, axis=0)
        weight = jnp.exp(scores - jnp.max(scores, axis=1, keepdims=True))
        probs = (weight / jnp.sum(weight, axis=1, keepdims=True)).astype(BF16)
        copies[c][1].wait()
        for i, t in enumerate(tokens):
            o = jnp.dot(probs[i * Q_HEADS : (i + 1) * Q_HEADS], v_ref[t], preferred_element_type=F32)
            picked = o[:, 0:HEAD]
            for k in range(1, KV_HEADS):
                picked = jnp.where(head_row >= GROUP * k, o[:, k * HEAD : (k + 1) * HEAD], picked)
            o_scr[t * Q_HEADS : (t + 1) * Q_HEADS, :] = picked
    for copy in late:
        copy.wait()
    squares = jnp.zeros((ROWS, HEAD), F32)
    hidden = []
    for h in range(Q_HEADS):
        span = slice(h * HEAD, (h + 1) * HEAD)
        part = (res_ref[:, span].astype(F32) + o_scr[pl.ds(h, ROWS, stride=Q_HEADS), :]).astype(BF16)
        hid_ref[:, span] = part
        part = part.astype(F32)
        squares = squares + part * part
        hidden.append(part)
    width = Q_HEADS * HEAD
    scale = lax.rsqrt(jnp.sum(squares, axis=1, keepdims=True) * (1.0 / width) + EPS)
    per = Q_HEADS // FEAT
    chunks = []
    for f in range(FEAT):
        heads = [
            (hidden[h] * scale * gain_ref[:, h * HEAD : (h + 1) * HEAD]).astype(BF16)
            for h in range(f * per, (f + 1) * per)
        ]
        chunks.append(jnp.concatenate(heads, axis=1))
    stacked = jnp.concatenate(chunks, axis=0)
    for s, out in enumerate(block_refs):
        picker = pick_scr[s * PACK : (s + 1) * PACK, :]
        out[...] = jnp.dot(picker, stacked, preferred_element_type=F32).astype(BF16)


def blend_kernel(plane_ref, ids_ref, gate_ref, out_ref):
    slot, spread, first, second = slots_of(plane_ref[0], ids_ref)
    gate = jnp.where(first, gate_ref[0:1, :], 0) + jnp.where(second, gate_ref[1:2, :], 0)
    high = jnp.dot((gate >> 6).astype(F32).astype(BF16), spread, preferred_element_type=F32)
    rest = jnp.dot((gate & 63).astype(F32).astype(BF16), spread, preferred_element_type=F32)
    for s in range(EXPERTS):
        match = matching(slot, s)
        rows = slice(s * PACK, (s + 1) * PACK)
        out_ref[rows, 0:LANES] = jnp.where(match, high[s : s + 1, :], 0.0).astype(BF16)
        out_ref[rows, LANES : 2 * LANES] = jnp.where(match, rest[s : s + 1, :], 0.0).astype(BF16)


def experts_kernel(slabs, *refs):
    blocks = refs[: slabs * EXPERTS]
    order_ref, back_ref, gate_ref, up_ref, down_ref = refs[slabs * EXPERTS : slabs * EXPERTS + 5]
    outs = refs[slabs * EXPERTS + 5 : -3]
    x_ref, a_ref, y_ref = refs[-3:]
    rows = EXPERTS * SLOTS
    part = y_ref.shape[2]
    order = order_ref[...]
    for q in range(slabs):
        packed = jnp.concatenate([b[...] for b in blocks[q * EXPERTS : (q + 1) * EXPERTS]], axis=0)
        x = jnp.dot(order, packed, preferred_element_type=F32).astype(BF16)
        for f in range(FEAT):
            x_ref[q * rows : (q + 1) * rows, f * part : (f + 1) * part] = x[f * rows : (f + 1) * rows]
    x = x_ref[...]
    units = gate_ref.shape[1]
    tile = min(512, units)
    for j in range(units // tile):
        span = slice(j * tile, (j + 1) * tile)
        g = jnp.dot(x, gate_ref[:, span], preferred_element_type=F32)
        u = jnp.dot(x, up_ref[:, span], preferred_element_type=F32)
        a_ref[:, span] = (g / (1.0 + jnp.exp(-g)) * u).astype(BF16)
    a = a_ref[...]
    for f in range(FEAT):
        span = slice(f * part, (f + 1) * part)
        y_ref[f] = jnp.dot(a, down_ref[:, span], preferred_element_type=F32).astype(BF16)
    back = back_ref[...]
    for q in range(slabs):
        stacked = jnp.concatenate([y_ref[f, q * rows : (q + 1) * rows, :] for f in range(FEAT)], axis=0)
        packed = jnp.dot(back, stacked, preferred_element_type=F32).astype(BF16)
        half = q // (slabs // 2)
        at = (q % (slabs // 2)) * EXPERTS * PACK
        outs[half][at : at + EXPERTS * PACK, :] = packed


def mix_kernel(hid_ref, blend_ref, m0_ref, m1_ref, m2_ref, m3_ref, out_ref):
    part = m0_ref.shape[1]
    packed = jnp.concatenate([m0_ref[...], m1_ref[...], m2_ref[...], m3_ref[...]], axis=0)
    mixed = lax.dot_general(blend_ref[...], packed, (((0,), (0,)), ((), ())), preferred_element_type=F32)
    mixed = mixed[:LANES] * (1.0 / 64.0) + mixed[LANES:] * (1.0 / 4096.0)
    for f in range(FEAT):
        span = slice(f * part, (f + 1) * part)
        own = hid_ref[:, span].astype(F32) + mixed[f * ROWS : (f + 1) * ROWS]
        out_ref[:, span] = own.astype(BF16)


VMEM = pl.BlockSpec(memory_space=pltpu.VMEM)
SMEM = pl.BlockSpec(memory_space=pltpu.SMEM)
HBM = pl.BlockSpec(memory_space=pltpu.HBM)


def params(mib):
    return pltpu.CompilerParams(vmem_limit_bytes=mib * MIB)


def attention(plane, *operands):
    width, kv_width = operands[1].shape[1], operands[3].shape[2]
    block = jax.ShapeDtypeStruct((PACK, width // FEAT), BF16)
    pinned = [pltpu.with_memory_space_constraint(x, pltpu.HBM) for x in operands]
    return pl.pallas_call(
        attention_kernel,
        out_shape=[jax.ShapeDtypeStruct((ROWS, width), BF16)] + [block] * EXPERTS,
        in_specs=[SMEM] + [HBM] * len(operands),
        out_specs=[VMEM] * (1 + EXPERTS),
        scratch_shapes=[pltpu.SMEM(operands[0].shape, I32)]
        + [pltpu.VMEM(x.shape, x.dtype) for x in operands[1:3]]
        + [pltpu.VMEM((ROWS, CACHE + ROWS, kv_width), BF16)] * 2
        + [pltpu.VMEM(x.shape, x.dtype) for x in operands[5:]]
        + [
            pltpu.VMEM((ROWS * Q_HEADS, HEAD), F32),
            pltpu.VMEM((ROWS * Q_HEADS, HEAD), F32),
            pltpu.VMEM((EXPERTS * PACK, LANES), BF16),
            pltpu.SemaphoreType.DMA((2, 1)),
            pltpu.SemaphoreType.DMA((7,)),
        ],
        compiler_params=params(6),
        cost_estimate=pl.CostEstimate(flops=40 * 10**9, bytes_accessed=4 * 10**6, transcendentals=0),
        name="attention",
    )(plane, *pinned)


def add_kernel(at, keep_ref, came_ref, out_ref):
    rows = out_ref.shape[0]
    out_ref[...] = (keep_ref[at : at + rows, :].astype(F32) + came_ref[...].astype(F32)).astype(BF16)


def add_block(keep, came, at):
    return pl.pallas_call(
        functools.partial(add_kernel, at),
        out_shape=jax.ShapeDtypeStruct(came.shape, BF16),
        in_specs=[VMEM] * 2,
        out_specs=VMEM,
        compiler_params=params(4),
        name="add_block",
    )(keep, came)


def local(
    queries, residual, key_cache, value_cache, new_keys, new_values, cache_len, norm_gain,
    expert_ids, gate_fixed, gate_weight, up_weight, down_weight,
):
    devices = lax.axis_size("attn")
    splits = devices // EXPERTS
    width = queries.shape[1]
    part = width // FEAT
    plane = (lax.axis_index("attn") // splits).astype(I32).reshape(1)
    ids, gates = expert_ids.T, gate_fixed.T
    hidden, *blocks = attention(
        plane, cache_len, queries, residual, key_cache, value_cache, new_keys, new_values,
        norm_gain.reshape(1, width), ids,
    )
    blend = pl.pallas_call(
        blend_kernel,
        out_shape=jax.ShapeDtypeStruct((EXPERTS * PACK, 2 * LANES), BF16),
        in_specs=[SMEM, VMEM, VMEM],
        out_specs=VMEM,
        compiler_params=params(4),
        name="blend",
    )(plane, ids, gates)

    def shifted(x, s):
        return lax.ppermute(x, "attn", [(i, (i + s * splits) % devices) for i in range(devices)])

    def swapped(x, bit):
        return lax.ppermute(x, "attn", [(i, i ^ bit) for i in range(devices)])

    got = [blocks[0]] + [shifted(blocks[s], s) for s in range(1, EXPERTS)]
    bit = splits // 2
    while bit >= 1:
        got = got + [swapped(b, bit) for b in got]
        bit //= 2
    total = splits * EXPERTS * SLOTS
    to = np.arange(EXPERTS * PACK)
    f, s, j = to // (EXPERTS * SLOTS), to // SLOTS % EXPERTS, to % SLOTS
    order = np.zeros((EXPERTS * PACK, EXPERTS * PACK), np.float32)
    order[to, s * PACK + f * SLOTS + j] = 1.0
    weights = [pltpu.with_memory_space_constraint(w, pltpu.VMEM) for w in (gate_weight, up_weight, down_weight)]
    units = gate_weight.shape[1]
    keep, send = pl.pallas_call(
        functools.partial(experts_kernel, splits),
        out_shape=[jax.ShapeDtypeStruct((splits // 2 * EXPERTS * PACK, part), BF16)] * 2,
        in_specs=[VMEM] * (splits * EXPERTS + 5),
        out_specs=[VMEM] * 2,
        scratch_shapes=[
            pltpu.VMEM((total, width), BF16),
            pltpu.VMEM((total, units), BF16),
            pltpu.VMEM((FEAT, total, part), BF16),
        ],
        compiler_params=params(16 if total <= 192 else 36),
        cost_estimate=pl.CostEstimate(
            flops=6 * total * width * units, bytes_accessed=6 * width * units, transcendentals=0
        ),
        name="experts",
    )(*got, jnp.asarray(order, BF16), jnp.asarray(order.T, BF16), *weights)

    def plus(a, b):
        return (a.astype(F32) + b.astype(F32)).astype(BF16)

    keep = plus(keep, swapped(send, 1))
    rows, bit = keep.shape[0], 2
    while rows > EXPERTS * PACK * 2:
        keep = plus(keep[: rows // 2], swapped(keep[rows // 2 :], bit))
        rows, bit = rows // 2, bit * 2
    summed = [None] * EXPERTS
    came = {}
    for s in (2, 1, 3, 0):
        came[s] = swapped(keep[rows // 2 + s * PACK : rows // 2 + (s + 1) * PACK], bit)
    for s in (2, 1, 3, 0):
        summed[s] = add_block(keep, came[s], s * PACK)
    mine = [summed[0]] + [shifted(summed[s], -s) for s in range(1, EXPERTS)]
    return pl.pallas_call(
        mix_kernel,
        out_shape=jax.ShapeDtypeStruct((ROWS, width), BF16),
        in_specs=[VMEM] * (2 + EXPERTS),
        out_specs=VMEM,
        compiler_params=params(8),
        name="mix",
    )(hidden, blend, *mine)


def solution(mesh):
    rows = P(("groups", "attn"), None)
    cached = P(("groups", "attn"), None, None)
    in_specs = (
        rows, rows, cached, cached, rows, rows, P(("groups", "attn")), P(), rows, rows,
        P(None, "attn"), P(None, "attn"), P("attn", None),
    )
    return jax.shard_map(local, mesh=mesh, in_specs=in_specs, out_specs=rows, check_vma=False)
```

```python
import functools
import math

import jax
import jax.numpy as jnp
import numpy as np
from jax import lax
from jax.experimental import pallas as pl
from jax.experimental.pallas import tpu as pltpu
from jax.sharding import PartitionSpec as P

HEAD = 128
Q_HEADS = 24
KV_HEADS = 4
EXPERTS = 4
TOP = 2
MB_ROWS = 8
CACHE = 96
CAP = 6
EPS = 1e-05
FEAT = 4
ROWS = 16
SLOTS = CAP * ROWS // MB_ROWS
PACK = FEAT * SLOTS
GROUP = Q_HEADS // KV_HEADS
LANES = FEAT * ROWS
SHIFTS = (0, 1, 3, 2)
MIB = 2**20
BF16, F32, I32 = jnp.bfloat16, jnp.float32, jnp.int32


def iota(shape, dim):
    return lax.broadcasted_iota(I32, shape, dim)


def slots_of(plane, ids_ref):
    expert = (plane + iota((8, ROWS), 0)) & (EXPERTS - 1)
    first = ids_ref[0:1, :] == expert
    second = ids_ref[1:2, :] == expert
    named = jnp.where(first | second, 1.0, 0.0).astype(BF16)
    token, lane_token = iota((ROWS, LANES), 0), iota((ROWS, LANES), 1) & (ROWS - 1)
    spread = jnp.where(token == lane_token, 1.0, 0.0).astype(BF16)
    earlier = (token < lane_token) & ((token >> 3) == (lane_token >> 3))
    earlier = jnp.where(earlier, 1.0, 0.0).astype(BF16)
    named_wide = jnp.dot(named, spread, preferred_element_type=F32)
    rank = jnp.dot(named, earlier, preferred_element_type=F32).astype(I32)
    batch = (iota((8, LANES), 1) & (ROWS - 1)) >> 3
    slot = jnp.where(named_wide > 0.5, batch * CAP + rank, -1)
    return slot, spread, first, second


def matching(slot, s):
    row, lane = iota((PACK, LANES), 0), iota((PACK, LANES), 1)
    chunk = sum((row >= SLOTS * f).astype(I32) for f in range(1, FEAT))
    return (chunk == (lane >> 4)) & (slot[s : s + 1, :] == row - SLOTS * chunk)


def attention_kernel(plane_ref, *refs):
    operands, outs, scratch = refs[:9], refs[9:14], refs[14:]
    len_hbm, q_hbm, res_hbm, k_hbm, v_hbm, nk_hbm, nv_hbm, gain_hbm, ids_hbm = operands
    hid_ref, *block_refs = outs
    len_ref, q_ref, res_ref, k_ref, v_ref, nk_ref, nv_ref, gain_ref, ids_ref, q_scr, o_scr, pick_scr, sems, small = scratch
    parts = sems.shape[1]
    step = ROWS // parts

    def fetch(source, target, sem):
        copy = pltpu.make_async_copy(source, target, sem)
        copy.start()
        return copy

    early = [
        fetch(ids_hbm, ids_ref, small.at[0]),
        fetch(q_hbm, q_ref, small.at[1]),
        fetch(nk_hbm, nk_ref, small.at[2]),
        fetch(nv_hbm, nv_ref, small.at[3]),
        fetch(len_hbm, len_ref, small.at[4]),
    ]
    copies = []
    for c in range(parts):
        own = pl.ds(c * step, step)
        copies.append((
            fetch(k_hbm.at[own], k_ref.at[own, pl.ds(0, CACHE)], sems.at[0, c]),
            fetch(v_hbm.at[own], v_ref.at[own, pl.ds(0, CACHE)], sems.at[1, c]),
        ))
    late = [fetch(res_hbm, res_ref, small.at[5]), fetch(gain_hbm, gain_ref, small.at[6])]
    early[0].wait()
    slot, _, _, _ = slots_of(plane_ref[0], ids_ref)
    for s in range(EXPERTS):
        pick_scr[s * PACK : (s + 1) * PACK, :] = jnp.where(matching(slot, s), 1.0, 0.0).astype(BF16)
    early[1].wait()
    for h in range(Q_HEADS):
        q_scr[pl.ds(h, ROWS, stride=Q_HEADS), :] = q_ref[:, h * HEAD : (h + 1) * HEAD].astype(F32)
    for copy in early[2:]:
        copy.wait()
    nk, nv = nk_ref[...], nv_ref[...]
    for t in range(ROWS):
        k_ref[t, CACHE:, :] = nk
        v_ref[t, CACHE:, :] = nv
    row, col = iota((Q_HEADS, KV_HEADS * HEAD), 0), iota((Q_HEADS, KV_HEADS * HEAD), 1)
    reads = sum((row >= GROUP * k).astype(I32) for k in range(1, KV_HEADS)) == (col >> 7)
    head_row = iota((Q_HEADS, HEAD), 0)
    position = iota((Q_HEADS, CACHE + ROWS), 1)
    scaling = 1.0 / math.sqrt(HEAD)
    contract = (((1,), (1,)), ((), ()))
    for c in range(parts):
        tokens = range(c * step, (c + 1) * step)
        copies[c][0].wait()
        scores = []
        for t in tokens:
            q = q_scr[t * Q_HEADS : (t + 1) * Q_HEADS, :]
            q = jnp.where(reads, jnp.concatenate([q] * KV_HEADS, axis=1), 0.0).astype(BF16)
            score = lax.dot_general(q, k_ref[t], contract, preferred_element_type=F32) * scaling
            live = (position < len_ref[t]) | (position == CACHE + t)
            scores.append(jnp.where(live, score, -1e30))
        scores = jnp.concatenate(scores, axis=0)
        weight = jnp.exp(scores - jnp.max(scores, axis=1, keepdims=True))
        probs = (weight / jnp.sum(weight, axis=1, keepdims=True)).astype(BF16)
        copies[c][1].wait()
        for i, t in enumerate(tokens):
            o = jnp.dot(probs[i * Q_HEADS : (i + 1) * Q_HEADS], v_ref[t], preferred_element_type=F32)
            picked = o[:, 0:HEAD]
            for k in range(1, KV_HEADS):
                picked = jnp.where(head_row >= GROUP * k, o[:, k * HEAD : (k + 1) * HEAD], picked)
            o_scr[t * Q_HEADS : (t + 1) * Q_HEADS, :] = picked
    for copy in late:
        copy.wait()
    squares = jnp.zeros((ROWS, HEAD), F32)
    hidden = []
    for h in range(Q_HEADS):
        span = slice(h * HEAD, (h + 1) * HEAD)
        part = (res_ref[:, span].astype(F32) + o_scr[pl.ds(h, ROWS, stride=Q_HEADS), :]).astype(BF16)
        hid_ref[:, span] = part
        part = part.astype(F32)
        squares = squares + part * part
        hidden.append(part)
    width = Q_HEADS * HEAD
    scale = lax.rsqrt(jnp.sum(squares, axis=1, keepdims=True) * (1.0 / width) + EPS)
    per = Q_HEADS // FEAT
    chunks = []
    for f in range(FEAT):
        heads = [
            (hidden[h] * scale * gain_ref[:, h * HEAD : (h + 1) * HEAD]).astype(BF16)
            for h in range(f * per, (f + 1) * per)
        ]
        chunks.append(jnp.concatenate(heads, axis=1))
    stacked = jnp.concatenate(chunks, axis=0)
    for s, out in enumerate(block_refs):
        picker = pick_scr[s * PACK : (s + 1) * PACK, :]
        out[...] = jnp.dot(picker, stacked, preferred_element_type=F32).astype(BF16)


def blend_kernel(plane_ref, ids_ref, gate_ref, out_ref):
    slot, spread, first, second = slots_of(plane_ref[0], ids_ref)
    gate = jnp.where(first, gate_ref[0:1, :], 0) + jnp.where(second, gate_ref[1:2, :], 0)
    high = jnp.dot((gate >> 6).astype(F32).astype(BF16), spread, preferred_element_type=F32)
    rest = jnp.dot((gate & 63).astype(F32).astype(BF16), spread, preferred_element_type=F32)
    for s in range(EXPERTS):
        match = matching(slot, s)
        rows = slice(s * PACK, (s + 1) * PACK)
        out_ref[rows, 0:LANES] = jnp.where(match, high[s : s + 1, :], 0.0).astype(BF16)
        out_ref[rows, LANES : 2 * LANES] = jnp.where(match, rest[s : s + 1, :], 0.0).astype(BF16)


def slab_kernel(order_ref, *refs):
    parts = dict(zip(SHIFTS, refs[:EXPERTS]))
    packed = jnp.concatenate([parts[s][...] for s in range(EXPERTS)], axis=0)
    refs[EXPERTS][...] = jnp.dot(order_ref[...], packed, preferred_element_type=F32).astype(BF16)


def experts_kernel(slabs, *refs):
    joined = refs[:slabs]
    gate_ref, up_ref, down_ref = refs[slabs : slabs + 3]
    outs = refs[slabs + 3 : slabs + 5]
    x_ref, a_ref = refs[slabs + 5 :]
    rows = EXPERTS * SLOTS
    part = joined[0].shape[1]
    for q in range(slabs):
        for f in range(FEAT):
            x_ref[q * rows : (q + 1) * rows, f * part : (f + 1) * part] = joined[q][f * rows : (f + 1) * rows, :]
    x = x_ref[...]
    units = gate_ref.shape[1]
    tile = min(512, units)
    for j in range(units // tile):
        span = slice(j * tile, (j + 1) * tile)
        g = jnp.dot(x, gate_ref[:, span], preferred_element_type=F32)
        u = jnp.dot(x, up_ref[:, span], preferred_element_type=F32)
        a_ref[:, span] = (g / (1.0 + jnp.exp(-g)) * u).astype(BF16)
    a = a_ref[...]
    for f in range(FEAT):
        span = slice(f * part, (f + 1) * part)
        y = jnp.dot(a, down_ref[:, span], preferred_element_type=F32).astype(BF16)
        for q in range(slabs):
            half = q // (slabs // 2)
            at = (q % (slabs // 2)) * EXPERTS * PACK + f * rows
            outs[half][at : at + rows, :] = y[q * rows : (q + 1) * rows]


def add_pack_kernel(back_ref, keep_ref, came_ref, out_ref):
    slab = EXPERTS * PACK
    for q in range(2):
        rows = slice(q * slab, (q + 1) * slab)
        total = (keep_ref[rows, :].astype(F32) + came_ref[rows, :].astype(F32)).astype(BF16)
        out_ref[rows, :] = jnp.dot(back_ref[...], total, preferred_element_type=F32).astype(BF16)


def mix_kernel(hid_ref, blend_ref, m0_ref, m1_ref, m2_ref, m3_ref, out_ref):
    part = m0_ref.shape[1]
    packed = jnp.concatenate([m0_ref[...], m1_ref[...], m2_ref[...], m3_ref[...]], axis=0)
    mixed = lax.dot_general(blend_ref[...], packed, (((0,), (0,)), ((), ())), preferred_element_type=F32)
    mixed = mixed[:LANES] * (1.0 / 64.0) + mixed[LANES:] * (1.0 / 4096.0)
    for f in range(FEAT):
        span = slice(f * part, (f + 1) * part)
        own = hid_ref[:, span].astype(F32) + mixed[f * ROWS : (f + 1) * ROWS]
        out_ref[:, span] = own.astype(BF16)


VMEM = pl.BlockSpec(memory_space=pltpu.VMEM)
SMEM = pl.BlockSpec(memory_space=pltpu.SMEM)
HBM = pl.BlockSpec(memory_space=pltpu.HBM)


def params(mib):
    return pltpu.CompilerParams(vmem_limit_bytes=mib * MIB)


def attention(plane, *operands):
    width, kv_width = operands[1].shape[1], operands[3].shape[2]
    block = jax.ShapeDtypeStruct((PACK, width // FEAT), BF16)
    pinned = [pltpu.with_memory_space_constraint(x, pltpu.HBM) for x in operands]
    return pl.pallas_call(
        attention_kernel,
        out_shape=[jax.ShapeDtypeStruct((ROWS, width), BF16)] + [block] * EXPERTS,
        in_specs=[SMEM] + [HBM] * len(operands),
        out_specs=[VMEM] * (1 + EXPERTS),
        scratch_shapes=[pltpu.SMEM(operands[0].shape, I32)]
        + [pltpu.VMEM(x.shape, x.dtype) for x in operands[1:3]]
        + [pltpu.VMEM((ROWS, CACHE + ROWS, kv_width), BF16)] * 2
        + [pltpu.VMEM(x.shape, x.dtype) for x in operands[5:]]
        + [
            pltpu.VMEM((ROWS * Q_HEADS, HEAD), F32),
            pltpu.VMEM((ROWS * Q_HEADS, HEAD), F32),
            pltpu.VMEM((EXPERTS * PACK, LANES), BF16),
            pltpu.SemaphoreType.DMA((2, 1)),
            pltpu.SemaphoreType.DMA((7,)),
        ],
        compiler_params=params(6),
        cost_estimate=pl.CostEstimate(flops=40 * 10**9, bytes_accessed=4 * 10**6, transcendentals=0),
        name="attention",
    )(plane, *pinned)


def add_kernel(at, keep_ref, came_ref, out_ref):
    rows = out_ref.shape[0]
    out_ref[...] = (keep_ref[at : at + rows, :].astype(F32) + came_ref[...].astype(F32)).astype(BF16)


def add_block(keep, came, at):
    return pl.pallas_call(
        functools.partial(add_kernel, at),
        out_shape=jax.ShapeDtypeStruct(came.shape, BF16),
        in_specs=[VMEM] * 2,
        out_specs=VMEM,
        compiler_params=params(4),
        name="add_block",
    )(keep, came)


def local(
    queries, residual, key_cache, value_cache, new_keys, new_values, cache_len, norm_gain,
    expert_ids, gate_fixed, gate_weight, up_weight, down_weight,
):
    devices = lax.axis_size("attn")
    splits = devices // EXPERTS
    width = queries.shape[1]
    part = width // FEAT
    plane = (lax.axis_index("attn") // splits).astype(I32).reshape(1)
    ids, gates = expert_ids.T, gate_fixed.T
    hidden, *blocks = attention(
        plane, cache_len, queries, residual, key_cache, value_cache, new_keys, new_values,
        norm_gain.reshape(1, width), ids,
    )
    blend = pl.pallas_call(
        blend_kernel,
        out_shape=jax.ShapeDtypeStruct((EXPERTS * PACK, 2 * LANES), BF16),
        in_specs=[SMEM, VMEM, VMEM],
        out_specs=VMEM,
        compiler_params=params(4),
        name="blend",
    )(plane, ids, gates)

    def shifted(x, s):
        return lax.ppermute(x, "attn", [(i, (i + s * splits) % devices) for i in range(devices)])

    def swapped(x, bit):
        return lax.ppermute(x, "attn", [(i, i ^ bit) for i in range(devices)])

    to = np.arange(EXPERTS * PACK)
    f, s, j = to // (EXPERTS * SLOTS), to // SLOTS % EXPERTS, to % SLOTS
    order = np.zeros((EXPERTS * PACK, EXPERTS * PACK), np.float32)
    order[to, s * PACK + f * SLOTS + j] = 1.0
    back = jnp.asarray(order.T, BF16)
    order = jnp.asarray(order, BF16)
    slab = jax.ShapeDtypeStruct((EXPERTS * PACK, part), BF16)

    def joined(group):
        return pl.pallas_call(
            slab_kernel, out_shape=slab, in_specs=[VMEM] * (1 + EXPERTS), out_specs=VMEM,
            compiler_params=params(4), name="slab",
        )(order, *group)

    got = [blocks[0]] + [shifted(blocks[s], s) for s in SHIFTS[1:]]
    bit = splits // 2
    while bit >= 2:
        got = got + [swapped(b, bit) for b in got]
        bit //= 2
    slabs = [joined(got[i : i + EXPERTS]) for i in range(0, len(got), EXPERTS)]
    slabs = slabs + [swapped(b, 1) for b in slabs]
    total = splits * EXPERTS * SLOTS
    weights = [pltpu.with_memory_space_constraint(w, pltpu.VMEM) for w in (gate_weight, up_weight, down_weight)]
    units = gate_weight.shape[1]
    keep, send = pl.pallas_call(
        functools.partial(experts_kernel, splits),
        out_shape=[jax.ShapeDtypeStruct((splits // 2 * EXPERTS * PACK, part), BF16)] * 2,
        in_specs=[VMEM] * (splits + 3),
        out_specs=[VMEM] * 2,
        scratch_shapes=[pltpu.VMEM((total, width), BF16), pltpu.VMEM((total, units), BF16)],
        compiler_params=params(16 if total <= 192 else 36),
        cost_estimate=pl.CostEstimate(
            flops=6 * total * width * units, bytes_accessed=6 * width * units, transcendentals=0
        ),
        name="experts",
    )(*slabs, *weights)

    came = swapped(send, 1)
    rows, bit = keep.shape[0], 2
    while rows > EXPERTS * PACK * 2:
        both = (keep.astype(F32) + came.astype(F32)).astype(BF16)
        keep, came = both[: rows // 2], swapped(both[rows // 2 :], bit)
        rows, bit = rows // 2, bit * 2
    keep = pl.pallas_call(
        add_pack_kernel, out_shape=jax.ShapeDtypeStruct((rows, part), BF16), in_specs=[VMEM] * 3,
        out_specs=VMEM, compiler_params=params(6), name="add_pack",
    )(back, keep, came)
    summed = [None] * EXPERTS
    came = {}
    for s in (2, 1, 3, 0):
        came[s] = swapped(keep[rows // 2 + s * PACK : rows // 2 + (s + 1) * PACK], bit)
    for s in (2, 1, 3, 0):
        summed[s] = add_block(keep, came[s], s * PACK)
    mine = [summed[0]] + [shifted(summed[s], -s) for s in range(1, EXPERTS)]
    return pl.pallas_call(
        mix_kernel,
        out_shape=jax.ShapeDtypeStruct((ROWS, width), BF16),
        in_specs=[VMEM] * (2 + EXPERTS),
        out_specs=VMEM,
        compiler_params=params(8),
        name="mix",
    )(hidden, blend, *mine)


def solution(mesh):
    rows = P(("groups", "attn"), None)
    cached = P(("groups", "attn"), None, None)
    in_specs = (
        rows, rows, cached, cached, rows, rows, P(("groups", "attn")), P(), rows, rows,
        P(None, "attn"), P(None, "attn"), P("attn", None),
    )
    return jax.shard_map(local, mesh=mesh, in_specs=in_specs, out_specs=rows, check_vma=False)
```

```python
import functools
import math

import jax
import jax.numpy as jnp
import numpy as np
from jax import lax
from jax.experimental import pallas as pl
from jax.experimental.pallas import tpu as pltpu
from jax.sharding import PartitionSpec as P

HEAD = 128
Q_HEADS = 24
KV_HEADS = 4
EXPERTS = 4
TOP = 2
MB_ROWS = 8
CACHE = 96
CAP = 6
EPS = 1e-05
FEAT = 4
ROWS = 16
SLOTS = CAP * ROWS // MB_ROWS
PACK = FEAT * SLOTS
GROUP = Q_HEADS // KV_HEADS
LANES = FEAT * ROWS
SHIFTS = (0, 1, 3, 2)
MIB = 2**20
BF16, F32, I32 = jnp.bfloat16, jnp.float32, jnp.int32


def iota(shape, dim):
    return lax.broadcasted_iota(I32, shape, dim)


def slots_of(plane, ids_ref):
    expert = (plane + iota((8, ROWS), 0)) & (EXPERTS - 1)
    first = ids_ref[0:1, :] == expert
    second = ids_ref[1:2, :] == expert
    named = jnp.where(first | second, 1.0, 0.0).astype(BF16)
    token, lane_token = iota((ROWS, LANES), 0), iota((ROWS, LANES), 1) & (ROWS - 1)
    spread = jnp.where(token == lane_token, 1.0, 0.0).astype(BF16)
    earlier = (token < lane_token) & ((token >> 3) == (lane_token >> 3))
    earlier = jnp.where(earlier, 1.0, 0.0).astype(BF16)
    named_wide = jnp.dot(named, spread, preferred_element_type=F32)
    rank = jnp.dot(named, earlier, preferred_element_type=F32).astype(I32)
    batch = (iota((8, LANES), 1) & (ROWS - 1)) >> 3
    slot = jnp.where(named_wide > 0.5, batch * CAP + rank, -1)
    return slot, spread, first, second


def matching(slot, s):
    row, lane = iota((PACK, LANES), 0), iota((PACK, LANES), 1)
    chunk = sum((row >= SLOTS * f).astype(I32) for f in range(1, FEAT))
    return (chunk == (lane >> 4)) & (slot[s : s + 1, :] == row - SLOTS * chunk)


def attention_kernel(plane_ref, *refs):
    operands, outs, scratch = refs[:9], refs[9:14], refs[14:]
    len_hbm, q_hbm, res_hbm, k_hbm, v_hbm, nk_hbm, nv_hbm, gain_hbm, ids_hbm = operands
    hid_ref, *block_refs = outs
    len_ref, q_ref, res_ref, k_ref, v_ref, nk_ref, nv_ref, gain_ref, ids_ref, q_scr, o_scr, pick_scr, sems, small = scratch
    parts = sems.shape[1]
    step = ROWS // parts

    def fetch(source, target, sem):
        copy = pltpu.make_async_copy(source, target, sem)
        copy.start()
        return copy

    early = [
        fetch(ids_hbm, ids_ref, small.at[0]),
        fetch(q_hbm, q_ref, small.at[1]),
        fetch(nk_hbm, nk_ref, small.at[2]),
        fetch(nv_hbm, nv_ref, small.at[3]),
        fetch(len_hbm, len_ref, small.at[4]),
    ]
    copies = []
    for c in range(parts):
        own = pl.ds(c * step, step)
        copies.append((
            fetch(k_hbm.at[own], k_ref.at[own, pl.ds(0, CACHE)], sems.at[0, c]),
            fetch(v_hbm.at[own], v_ref.at[own, pl.ds(0, CACHE)], sems.at[1, c]),
        ))
    late = [fetch(res_hbm, res_ref, small.at[5]), fetch(gain_hbm, gain_ref, small.at[6])]
    early[0].wait()
    slot, _, _, _ = slots_of(plane_ref[0], ids_ref)
    for s in range(EXPERTS):
        pick_scr[s * PACK : (s + 1) * PACK, :] = jnp.where(matching(slot, s), 1.0, 0.0).astype(BF16)
    early[1].wait()
    for h in range(Q_HEADS):
        q_scr[pl.ds(h, ROWS, stride=Q_HEADS), :] = q_ref[:, h * HEAD : (h + 1) * HEAD].astype(F32)
    for copy in early[2:]:
        copy.wait()
    nk, nv = nk_ref[...], nv_ref[...]
    for t in range(ROWS):
        k_ref[t, CACHE:, :] = nk
        v_ref[t, CACHE:, :] = nv
    row, col = iota((Q_HEADS, KV_HEADS * HEAD), 0), iota((Q_HEADS, KV_HEADS * HEAD), 1)
    reads = sum((row >= GROUP * k).astype(I32) for k in range(1, KV_HEADS)) == (col >> 7)
    head_row = iota((Q_HEADS, HEAD), 0)
    position = iota((Q_HEADS, CACHE + ROWS), 1)
    scaling = 1.0 / math.sqrt(HEAD)
    contract = (((1,), (1,)), ((), ()))
    for c in range(parts):
        tokens = range(c * step, (c + 1) * step)
        copies[c][0].wait()
        scores = []
        for t in tokens:
            q = q_scr[t * Q_HEADS : (t + 1) * Q_HEADS, :]
            q = jnp.where(reads, jnp.concatenate([q] * KV_HEADS, axis=1), 0.0).astype(BF16)
            score = lax.dot_general(q, k_ref[t], contract, preferred_element_type=F32) * scaling
            live = (position < len_ref[t]) | (position == CACHE + t)
            scores.append(jnp.where(live, score, -1e30))
        scores = jnp.concatenate(scores, axis=0)
        weight = jnp.exp(scores - jnp.max(scores, axis=1, keepdims=True))
        probs = (weight / jnp.sum(weight, axis=1, keepdims=True)).astype(BF16)
        copies[c][1].wait()
        for i, t in enumerate(tokens):
            o = jnp.dot(probs[i * Q_HEADS : (i + 1) * Q_HEADS], v_ref[t], preferred_element_type=F32)
            picked = o[:, 0:HEAD]
            for k in range(1, KV_HEADS):
                picked = jnp.where(head_row >= GROUP * k, o[:, k * HEAD : (k + 1) * HEAD], picked)
            o_scr[t * Q_HEADS : (t + 1) * Q_HEADS, :] = picked
    for copy in late:
        copy.wait()
    squares = jnp.zeros((ROWS, HEAD), F32)
    hidden = []
    for h in range(Q_HEADS):
        span = slice(h * HEAD, (h + 1) * HEAD)
        part = (res_ref[:, span].astype(F32) + o_scr[pl.ds(h, ROWS, stride=Q_HEADS), :]).astype(BF16)
        hid_ref[:, span] = part
        part = part.astype(F32)
        squares = squares + part * part
        hidden.append(part)
    width = Q_HEADS * HEAD
    scale = lax.rsqrt(jnp.sum(squares, axis=1, keepdims=True) * (1.0 / width) + EPS)
    per = Q_HEADS // FEAT
    chunks = []
    for f in range(FEAT):
        heads = [
            (hidden[h] * scale * gain_ref[:, h * HEAD : (h + 1) * HEAD]).astype(BF16)
            for h in range(f * per, (f + 1) * per)
        ]
        chunks.append(jnp.concatenate(heads, axis=1))
    stacked = jnp.concatenate(chunks, axis=0)
    for s, out in enumerate(block_refs):
        picker = pick_scr[s * PACK : (s + 1) * PACK, :]
        out[...] = jnp.dot(picker, stacked, preferred_element_type=F32).astype(BF16)


def blend_kernel(plane_ref, ids_ref, gate_ref, out_ref, wide_ref):
    slot, spread, first, second = slots_of(plane_ref[0], ids_ref)
    gate = jnp.where(first, gate_ref[0:1, :], 0) + jnp.where(second, gate_ref[1:2, :], 0)
    high = jnp.dot((gate >> 6).astype(F32).astype(BF16), spread, preferred_element_type=F32)
    rest = jnp.dot((gate & 63).astype(F32).astype(BF16), spread, preferred_element_type=F32)
    for s in range(EXPERTS):
        match = matching(slot, s)
        rows = slice(s * PACK, (s + 1) * PACK)
        both = [jnp.where(match, high[s : s + 1, :], 0.0), jnp.where(match, rest[s : s + 1, :], 0.0)]
        wide_ref[rows, :] = jnp.concatenate(both, axis=1)
    out_ref[...] = wide_ref[...].T.astype(BF16)


def slab_kernel(order_ref, *refs):
    parts = dict(zip(SHIFTS, refs[:EXPERTS]))
    packed = jnp.concatenate([parts[s][...] for s in range(EXPERTS)], axis=0)
    refs[EXPERTS][...] = jnp.dot(order_ref[...], packed, preferred_element_type=F32).astype(BF16)


def experts_kernel(slabs, *refs):
    joined = refs[:slabs]
    gate_ref, up_ref, down_ref = refs[slabs : slabs + 3]
    outs = refs[slabs + 3 : slabs + 5]
    x_ref, a_ref = refs[slabs + 5 :]
    rows = EXPERTS * SLOTS
    part = joined[0].shape[1]
    for q in range(slabs):
        for f in range(FEAT):
            x_ref[q * rows : (q + 1) * rows, f * part : (f + 1) * part] = joined[q][f * rows : (f + 1) * rows, :]
    x = x_ref[...]
    units = gate_ref.shape[1]
    tile = min(512, units)
    for j in range(units // tile):
        span = slice(j * tile, (j + 1) * tile)
        g = jnp.dot(x, gate_ref[:, span], preferred_element_type=F32)
        u = jnp.dot(x, up_ref[:, span], preferred_element_type=F32)
        a_ref[:, span] = (g / (1.0 + jnp.exp(-g)) * u).astype(BF16)
    a = a_ref[...]
    for f in range(FEAT):
        span = slice(f * part, (f + 1) * part)
        y = jnp.dot(a, down_ref[:, span], preferred_element_type=F32).astype(BF16)
        for q in range(slabs):
            half = q // (slabs // 2)
            at = (q % (slabs // 2)) * EXPERTS * PACK + f * rows
            outs[half][at : at + rows, :] = y[q * rows : (q + 1) * rows]


def add_pack_kernel(at, back_ref, keep_ref, came_ref, out_ref):
    rows = slice(at, at + EXPERTS * PACK)
    total = (keep_ref[rows, :].astype(F32) + came_ref[rows, :].astype(F32)).astype(BF16)
    out_ref[...] = jnp.dot(back_ref[...], total, preferred_element_type=F32).astype(BF16)


def mix_kernel(hid_ref, blend_ref, m0_ref, m1_ref, m2_ref, m3_ref, out_ref):
    part = m0_ref.shape[1]
    packed = jnp.concatenate([m0_ref[...], m1_ref[...], m2_ref[...], m3_ref[...]], axis=0)
    mixed = jnp.dot(blend_ref[...], packed, preferred_element_type=F32)
    mixed = mixed[:LANES] * (1.0 / 64.0) + mixed[LANES:] * (1.0 / 4096.0)
    for f in range(FEAT):
        span = slice(f * part, (f + 1) * part)
        own = hid_ref[:, span].astype(F32) + mixed[f * ROWS : (f + 1) * ROWS]
        out_ref[:, span] = own.astype(BF16)


VMEM = pl.BlockSpec(memory_space=pltpu.VMEM)
SMEM = pl.BlockSpec(memory_space=pltpu.SMEM)
HBM = pl.BlockSpec(memory_space=pltpu.HBM)


def params(mib):
    return pltpu.CompilerParams(vmem_limit_bytes=mib * MIB)


def attention(plane, *operands):
    width, kv_width = operands[1].shape[1], operands[3].shape[2]
    block = jax.ShapeDtypeStruct((PACK, width // FEAT), BF16)
    pinned = [pltpu.with_memory_space_constraint(x, pltpu.HBM) for x in operands]
    return pl.pallas_call(
        attention_kernel,
        out_shape=[jax.ShapeDtypeStruct((ROWS, width), BF16)] + [block] * EXPERTS,
        in_specs=[SMEM] + [HBM] * len(operands),
        out_specs=[VMEM] * (1 + EXPERTS),
        scratch_shapes=[pltpu.SMEM(operands[0].shape, I32)]
        + [pltpu.VMEM(x.shape, x.dtype) for x in operands[1:3]]
        + [pltpu.VMEM((ROWS, CACHE + ROWS, kv_width), BF16)] * 2
        + [pltpu.VMEM(x.shape, x.dtype) for x in operands[5:]]
        + [
            pltpu.VMEM((ROWS * Q_HEADS, HEAD), F32),
            pltpu.VMEM((ROWS * Q_HEADS, HEAD), F32),
            pltpu.VMEM((EXPERTS * PACK, LANES), BF16),
            pltpu.SemaphoreType.DMA((2, 1)),
            pltpu.SemaphoreType.DMA((7,)),
        ],
        compiler_params=params(6),
        cost_estimate=pl.CostEstimate(flops=40 * 10**9, bytes_accessed=4 * 10**6, transcendentals=0),
        name="attention",
    )(plane, *pinned)


def add_kernel(at, keep_ref, came_ref, out_ref):
    rows = out_ref.shape[0]
    out_ref[...] = (keep_ref[at : at + rows, :].astype(F32) + came_ref[...].astype(F32)).astype(BF16)


def add_block(keep, came, at):
    return pl.pallas_call(
        functools.partial(add_kernel, at),
        out_shape=jax.ShapeDtypeStruct(came.shape, BF16),
        in_specs=[VMEM] * 2,
        out_specs=VMEM,
        compiler_params=params(4),
        name="add_block",
    )(keep, came)


def local(
    queries, residual, key_cache, value_cache, new_keys, new_values, cache_len, norm_gain,
    expert_ids, gate_fixed, gate_weight, up_weight, down_weight,
):
    devices = lax.axis_size("attn")
    splits = devices // EXPERTS
    width = queries.shape[1]
    part = width // FEAT
    plane = (lax.axis_index("attn") // splits).astype(I32).reshape(1)
    ids, gates = expert_ids.T, gate_fixed.T
    hidden, *blocks = attention(
        plane, cache_len, queries, residual, key_cache, value_cache, new_keys, new_values,
        norm_gain.reshape(1, width), ids,
    )
    blend = pl.pallas_call(
        blend_kernel,
        out_shape=jax.ShapeDtypeStruct((2 * LANES, EXPERTS * PACK), BF16),
        scratch_shapes=[pltpu.VMEM((EXPERTS * PACK, 2 * LANES), F32)],
        in_specs=[SMEM, VMEM, VMEM],
        out_specs=VMEM,
        compiler_params=params(4),
        name="blend",
    )(plane, ids, gates)

    def shifted(x, s):
        return lax.ppermute(x, "attn", [(i, (i + s * splits) % devices) for i in range(devices)])

    def swapped(x, bit):
        return lax.ppermute(x, "attn", [(i, i ^ bit) for i in range(devices)])

    to = np.arange(EXPERTS * PACK)
    f, s, j = to // (EXPERTS * SLOTS), to // SLOTS % EXPERTS, to % SLOTS
    order = np.zeros((EXPERTS * PACK, EXPERTS * PACK), np.float32)
    order[to, s * PACK + f * SLOTS + j] = 1.0
    back = jnp.asarray(order.T, BF16)
    order = jnp.asarray(order, BF16)
    slab = jax.ShapeDtypeStruct((EXPERTS * PACK, part), BF16)

    def joined(group):
        return pl.pallas_call(
            slab_kernel, out_shape=slab, in_specs=[VMEM] * (1 + EXPERTS), out_specs=VMEM,
            compiler_params=params(4), name="slab",
        )(order, *group)

    got = [blocks[0]] + [shifted(blocks[s], s) for s in SHIFTS[1:]]
    bit = splits // 2
    while bit >= 2:
        got = got + [swapped(b, bit) for b in got]
        bit //= 2
    slabs = [joined(got[i : i + EXPERTS]) for i in range(0, len(got), EXPERTS)]
    slabs = slabs + [swapped(b, 1) for b in slabs]
    total = splits * EXPERTS * SLOTS
    weights = [pltpu.with_memory_space_constraint(w, pltpu.VMEM) for w in (gate_weight, up_weight, down_weight)]
    units = gate_weight.shape[1]
    keep, send = pl.pallas_call(
        functools.partial(experts_kernel, splits),
        out_shape=[jax.ShapeDtypeStruct((splits // 2 * EXPERTS * PACK, part), BF16)] * 2,
        in_specs=[VMEM] * (splits + 3),
        out_specs=[VMEM] * 2,
        scratch_shapes=[pltpu.VMEM((total, width), BF16), pltpu.VMEM((total, units), BF16)],
        compiler_params=params(16 if total <= 192 else 36),
        cost_estimate=pl.CostEstimate(
            flops=6 * total * width * units, bytes_accessed=6 * width * units, transcendentals=0
        ),
        name="experts",
    )(*slabs, *weights)

    came = swapped(send, 1)
    rows, bit = keep.shape[0], 2
    while rows > EXPERTS * PACK * 2:
        both = (keep.astype(F32) + came.astype(F32)).astype(BF16)
        keep, came = both[: rows // 2], swapped(both[rows // 2 :], bit)
        rows, bit = rows // 2, bit * 2

    def add_pack(at):
        return pl.pallas_call(
            functools.partial(add_pack_kernel, at), out_shape=slab, in_specs=[VMEM] * 3, out_specs=VMEM,
            compiler_params=params(6), name="add_pack",
        )(back, keep, came)

    leaving, staying = add_pack(EXPERTS * PACK), add_pack(0)
    arrived = {s: swapped(leaving[s * PACK : (s + 1) * PACK], bit) for s in (2, 1, 3, 0)}
    summed = [add_block(staying, arrived[s], s * PACK) for s in range(EXPERTS)]
    mine = [summed[0]] + [shifted(summed[s], -s) for s in range(1, EXPERTS)]
    return pl.pallas_call(
        mix_kernel,
        out_shape=jax.ShapeDtypeStruct((ROWS, width), BF16),
        in_specs=[VMEM] * (2 + EXPERTS),
        out_specs=VMEM,
        compiler_params=params(8),
        name="mix",
    )(hidden, blend, *mine)


def solution(mesh):
    rows = P(("groups", "attn"), None)
    cached = P(("groups", "attn"), None, None)
    in_specs = (
        rows, rows, cached, cached, rows, rows, P(("groups", "attn")), P(), rows, rows,
        P(None, "attn"), P(None, "attn"), P("attn", None),
    )
    return jax.shard_map(local, mesh=mesh, in_specs=in_specs, out_specs=rows, check_vma=False)
```
